128 devices in a mesh: seq: 8 (over z_hi, x), tp: 16 (over y, z_lo, core).
Axes of the slice: x: 4, y: 4, z: 4 (z_hi: 2, z_lo: 2; z = z_hi * 2 + z_lo), core: 2. Of those that a mesh axis runs over, the one named last changes fastest.
Arguments:
- activations: bfloat16 [2048, 8192], P('seq', 'tp'), may hold values from -36 to 36
- norm_gain: bfloat16 [8192], P('tp'), may hold values from 0.099609375 to 1.8984375
- in_proj: bfloat16 [8192, 3, 4096], P(None, None, 'tp'), may hold values from -0.0625 to 0.0625
- short_taps: float32 [3, 3, 4096], P(None, None, 'tp'), may hold values from -3.5 to 3.5
- medium_taps: float32 [256, 128], P('tp'), may hold values from -0.5 to 0.5
- cotangent: bfloat16 [2048, 4096], P('seq', 'tp'), may hold values from -1.1953125 to 1.1953125
Outputs:
- mixer_out: bfloat16 [2048, 4096], P('seq', 'tp')
- grad_input: bfloat16 [2048, 8192], P('seq', 'tp')
- grad_proj: bfloat16 [8192, 3, 4096], P('seq', None, 'tp')
The draws below stay inside these ranges and needn't reach their ends.
All inputs are finite; a program needn't handle non-finite values.
Results may differ from the reference program's by a relative error of at most 0.02.
Values may be sent and summed in bfloat16 or wider, within the bound.
A program may use at most 192 MiB of HBM per device.

```python
import math
import jax
import jax.numpy as jnp
from jax import lax

D = 8192
C = 4096
GROUP = 16
LS = 3
LM = 128
TOK_DEV = 256
TOKENS = 2048
GROUPS = 256
N_SEQ = 8


def draw_activations(key, part):
    base_key = jax.random.fold_in(key, 11)
    column_key = jax.random.fold_in(key, 12)
    row_key = jax.random.fold_in(key, 13)
    base = jnp.clip(jax.random.normal(base_key, (TOKENS, D), jnp.float32), -4.0, 4.0)
    columns = jnp.exp(jax.random.uniform(column_key, (1, D), jnp.float32, math.log(0.3), math.log(3.0)))
    row_scale = jnp.exp(jax.random.uniform(row_key, (TOKENS, 1), jnp.float32, math.log(0.3), math.log(3.0)))
    return (base * columns * row_scale).astype(jnp.bfloat16)


def shard_levels(own_key, extent, shards, least, largest):
    loudness = 1.0
    for dim, parts in shards:
        steps = jax.random.uniform(jax.random.fold_in(jax.random.fold_in(own_key, 6), dim), (parts,), jnp.float32, least / len(shards), largest / len(shards))
        loudness = loudness * jnp.repeat(jnp.exp(steps), extent[dim] // parts).reshape((-1,) + (1,) * (len(extent) - 1 - dim))
    return loudness


def bell_draw(rng, extent, deviation, reach, cuts=(), dtype=jnp.bfloat16):
    loudness = shard_levels(rng, extent, cuts, -0.22, 0.18) if cuts else 1.0
    result = jax.random.normal(rng, extent, jnp.float32) * deviation * loudness
    return jnp.minimum(jnp.maximum(result, -reach), reach).astype(dtype)


def setup_inputs(seed: int = 0) -> dict:
    arg_keys = jax.random.split(jax.random.key(seed), 7)
    return {
        "activations": draw_activations(jax.random.fold_in(arg_keys[6], 71), 0),
        "norm_gain": jnp.clip(1.0 + 0.18 * jax.random.normal(arg_keys[1], (D,), jnp.float32), 0.099609375, 1.8984375).astype(jnp.bfloat16),
        "in_proj": bell_draw(arg_keys[2], (D, 3, C), D ** -0.5, 0.0625, ((2, 16),)),
        "short_taps": bell_draw(arg_keys[3], (LS, 3, C), LS ** -0.5, 3.5, ((2, 16),), jnp.float32),
        "medium_taps": bell_draw(arg_keys[4], (GROUPS, LM), LM ** -0.5, 0.5, ((0, 16),), jnp.float32),
        "cotangent": bell_draw(arg_keys[5], (TOKENS, C), 0.2, 1.1953125, ((0, 8), (1, 16))),
    }


norm_eps = 1e-06

def causal_short(source, taps):
    length = source.shape[0]
    padded = jnp.concatenate([jnp.zeros((LS - 1,) + source.shape[1:], jnp.float32), source.astype(jnp.float32)], 0)
    total = jnp.zeros(source.shape, jnp.float32)
    for index in range(LS):
        total = total + taps[index] * padded[LS - 1 - index:LS - 1 - index + length]
    return total

def anticausal_short(source, taps):
    length = source.shape[0]
    padded = jnp.concatenate([source.astype(jnp.float32), jnp.zeros((LS - 1,) + source.shape[1:], jnp.float32)], 0)
    total = jnp.zeros(source.shape, jnp.float32)
    for index in range(LS):
        total = total + taps[index] * padded[index:index + length]
    return total

def causal_medium(source, tap_table):
    length = source.shape[0]
    padded = jnp.concatenate([jnp.zeros((LM - 1, source.shape[1]), jnp.float32), source.astype(jnp.float32)], 0)

    def add_tap(index, total):
        where_from = (LM - 1 - index).astype(jnp.int32)
        window = lax.dynamic_slice_in_dim(padded, where_from, length, 0)
        column = lax.dynamic_slice_in_dim(tap_table, index.astype(jnp.int32), 1, 1)[:, 0]
        return total + column * window
    return lax.fori_loop(0, LM, add_tap, jnp.zeros(source.shape, jnp.float32))

def anticausal_medium(source, tap_table):
    length = source.shape[0]
    padded = jnp.concatenate([source.astype(jnp.float32), jnp.zeros((LM - 1, source.shape[1]), jnp.float32)], 0)

    def add_tap(index, total):
        window = lax.dynamic_slice_in_dim(padded, index.astype(jnp.int32), length, 0)
        column = lax.dynamic_slice_in_dim(tap_table, index.astype(jnp.int32), 1, 1)[:, 0]
        return total + column * window
    return lax.fori_loop(0, LM, add_tap, jnp.zeros(source.shape, jnp.float32))

def reference(activations, norm_gain, in_proj, short_taps, medium_taps, cotangent):
    act_float = activations.astype(jnp.float32)
    inv_rms = lax.rsqrt(lax.optimization_barrier(jnp.mean(act_float * act_float, axis=1, keepdims=True)) + norm_eps)
    scaled = act_float * inv_rms
    gain_float = norm_gain.astype(jnp.float32)
    normed = (scaled * gain_float).astype(jnp.bfloat16)
    weight = in_proj.reshape(D, 3 * C)
    projected = jnp.dot(normed, weight, preferred_element_type=jnp.float32).astype(jnp.bfloat16).reshape(TOKENS, 3, C)
    feat = causal_short(projected, short_taps).astype(jnp.bfloat16)
    gated = (feat[:, 1].astype(jnp.float32) * feat[:, 2].astype(jnp.float32)).astype(jnp.bfloat16)
    tap_table = jnp.repeat(medium_taps, GROUP, axis=0)
    filtered = causal_medium(gated, tap_table)
    mixer_out = (feat[:, 0].astype(jnp.float32) * filtered).astype(jnp.bfloat16)
    grad_out = cotangent.astype(jnp.float32)
    grad_filtered = (grad_out * feat[:, 0].astype(jnp.float32)).astype(jnp.bfloat16)
    grad_gated = anticausal_medium(grad_filtered, tap_table)
    grad_q = grad_out * filtered
    grad_k = grad_gated * feat[:, 2].astype(jnp.float32)
    grad_v = grad_gated * feat[:, 1].astype(jnp.float32)
    grad_feat = jnp.stack([grad_q, grad_k, grad_v], 1).astype(jnp.bfloat16)
    grad_pre = anticausal_short(grad_feat, short_taps).astype(jnp.bfloat16).reshape(TOKENS, 3 * C)
    grad_normed = jnp.dot(grad_pre, weight.T, preferred_element_type=jnp.float32)
    grad_scaled = gain_float * grad_normed
    stat = lax.optimization_barrier(jnp.mean(grad_scaled * scaled, axis=1, keepdims=True))
    grad_input = (inv_rms * (grad_scaled - scaled * stat)).astype(jnp.bfloat16)
    normed_slabs = normed.reshape(N_SEQ, TOK_DEV, D)
    grad_slabs = grad_pre.reshape(N_SEQ, TOK_DEV, 3 * C)

    def add_slab(total, pair):
        slab_norm, slab_grad = pair
        partial_sum = jnp.dot(slab_norm.T, slab_grad, preferred_element_type=jnp.float32).astype(jnp.bfloat16)
        partial_sum = lax.optimization_barrier(partial_sum)
        return (total + partial_sum.astype(jnp.float32), None)
    total, _ = lax.scan(add_slab, jnp.zeros((D, 3 * C), jnp.float32), (normed_slabs, grad_slabs))
    grad_proj = total.astype(jnp.bfloat16).reshape(D, 3, C)
    return (mixer_out, grad_input, grad_proj)
```

```python
import functools

import jax
import jax.numpy as jnp
from jax import lax
from jax.experimental import pallas as pl
from jax.experimental.pallas import tpu as pltpu
from jax.sharding import PartitionSpec as P

GROUP = 16
LM = 128
BLK = 128
EPS = 1e-06
F32 = jnp.float32
BF16 = jnp.bfloat16
MESH = pl.DeviceIdType.MESH


def build_bands(rows_ref, band_ref):
    def one(g, carry):
        row = jnp.broadcast_to(rows_ref[pl.ds(g, 1), :], (BLK, 2 * BLK))
        band_ref[g] = pltpu.roll(row, 0, 1, stride=1, stride_axis=0).astype(BF16)
        return carry

    lax.fori_loop(0, rows_ref.shape[0], one, 0)


def apply_band(band_ref, first, source_ref, row0):
    lane = lax.broadcasted_iota(jnp.int32, (BLK, 128), 1) // GROUP
    halves = source_ref.shape[1] // 128

    def one(g, totals):
        new = []
        for h in range(halves):
            part = jnp.dot(
                band_ref[first + h * 8 + g],
                source_ref[row0 : row0 + 2 * BLK, h * 128 : h * 128 + 128],
                preferred_element_type=F32,
            )
            new.append(jnp.where(lane == g, part, totals[h]))
        return tuple(new)

    totals = lax.fori_loop(0, 8, one, tuple(jnp.zeros((BLK, 128), F32) for _ in range(halves)))
    return jnp.concatenate(totals, 1)


def mixer(pre, cot, taps, band, mix, gp, ext, feat, gext, gfext, gft, ptail, ghead, gtail, send, recv):
    tok, ch = pre.shape[1], pre.shape[2]
    n = lax.axis_size("seq")
    me = lax.axis_index("seq")
    after, before = lax.rem(me + 1, n), lax.rem(me + n - 1, n)
    first, last = me == 0, me == n - 1
    groups = ch // GROUP

    def remote(src, dst, index, to):
        return pltpu.make_async_remote_copy(
            src_ref=src, dst_ref=dst, send_sem=send.at[index], recv_sem=recv.at[index],
            device_id={"seq": to}, device_id_type=MESH,
        )

    tail_copy = remote(pre.at[:, pl.ds(tok - 16, 16), :], ptail, 0, after)
    tail_copy.start()
    for j in range(3):
        ext[j, 8 : 8 + tok, :] = pre[j].astype(F32)

    def short(j, lo, hi):
        total = taps[0, j : j + 1, :] * ext[j, 8 + lo : 8 + hi, :]
        total += taps[1, j : j + 1, :] * ext[j, 7 + lo : 7 + hi, :]
        total += taps[2, j : j + 1, :] * ext[j, 6 + lo : 6 + hi, :]
        return total.astype(BF16)

    def gate(lo, hi):
        k, v = short(1, lo, hi), short(2, lo, hi)
        feat[1, lo:hi, :] = k
        feat[2, lo:hi, :] = v
        gext[BLK + lo : BLK + hi, :] = (k.astype(F32) * v.astype(F32)).astype(BF16)

    gate(tok - BLK, tok)
    gated_copy = remote(gext.at[pl.ds(tok, BLK), :], gext.at[pl.ds(0, BLK), :], 1, after)
    gated_copy.start()

    tail_copy.wait_recv()
    for j in range(3):
        ext[j, 0:8, :] = jnp.where(first, 0.0, ptail[j].astype(F32)[8:16])
    q = short(0, 0, tok)
    feat[0] = q
    grad_out = cot[...].astype(F32)
    gfext[0:tok, :] = (grad_out * q.astype(F32)).astype(BF16)
    filt_copy = remote(gfext.at[pl.ds(0, BLK), :], gtail, 2, before)
    filt_copy.start()
    gate(0, tok - BLK)

    def grad_kv(lo):
        gg = apply_band(band, groups, gfext, lo)
        gft[1, lo : lo + BLK, :] = (gg * feat[2, lo : lo + BLK, :].astype(F32)).astype(BF16).astype(F32)
        gft[2, lo : lo + BLK, :] = (gg * feat[1, lo : lo + BLK, :].astype(F32)).astype(BF16).astype(F32)

    def forward(lo):
        filt = apply_band(band, 0, gext, lo)
        mix[lo : lo + BLK, :] = (feat[0, lo : lo + BLK, :].astype(F32) * filt).astype(BF16)
        gft[0, lo : lo + BLK, :] = (cot[lo : lo + BLK, :].astype(F32) * filt).astype(BF16).astype(F32)

    grad_kv(0)
    gated_copy.wait_recv()

    @pl.when(first)
    def _():
        gext[0:BLK, :] = jnp.zeros((BLK, ch), BF16)

    forward(0)
    for j in range(3):
        ghead[0, j] = gft[j, 0:16, :].astype(BF16)
    head_copy = remote(ghead.at[0], ghead.at[1], 3, before)
    head_copy.start()
    forward(BLK)
    filt_copy.wait_recv()
    gfext[tok : tok + BLK, :] = jnp.where(last, 0.0, gtail[...].astype(F32)).astype(BF16)
    grad_kv(BLK)
    head_copy.wait_recv()
    for j in range(3):
        gft[j, tok : tok + 8, :] = jnp.where(last, 0.0, ghead[1, j].astype(F32)[0:8])
    for j in range(3):
        total = taps[0, j : j + 1, :] * gft[j, 0:tok, :]
        total += taps[1, j : j + 1, :] * gft[j, 1 : tok + 1, :]
        total += taps[2, j : j + 1, :] * gft[j, 2 : tok + 2, :]
        gp[j] = total.astype(BF16)
    for copy in (tail_copy, gated_copy, filt_copy, head_copy):
        copy.wait_send()


def mixer_scratch(tok, ch):
    return [
        pltpu.VMEM((2 * ch // GROUP, BLK, 2 * BLK), BF16),
        pltpu.VMEM((3, tok + 8, ch), F32),
        pltpu.VMEM((3, tok, ch), BF16),
        pltpu.VMEM((tok + BLK, ch), BF16),
        pltpu.VMEM((tok + BLK, ch), BF16),
        pltpu.VMEM((3, tok + 8, ch), F32),
        pltpu.VMEM((3, 16, ch), BF16),
        pltpu.VMEM((2, 3, 16, ch), BF16),
        pltpu.VMEM((BLK, ch), BF16),
        pltpu.SemaphoreType.DMA((4,)),
        pltpu.SemaphoreType.DMA((4,)),
    ]


def mixer_kernel(pre, cot, taps, rows, mix, gp, band, *scratch):
    n = lax.axis_size("seq")
    me = lax.axis_index("seq")
    barrier = pltpu.get_barrier_semaphore()
    for to in (lax.rem(me + 1, n), lax.rem(me + n - 1, n)):
        pl.semaphore_signal(barrier, inc=1, device_id={"seq": to}, device_id_type=MESH)
    build_bands(rows, band)
    pl.semaphore_wait(barrier, 2)
    mixer(pre, cot, taps, band, mix, gp, *scratch)


def band_rows(medium_taps):
    zero = jnp.zeros_like(medium_taps)
    forward = jnp.concatenate([zero[:, :1], medium_taps[:, ::-1], zero[:, 1:]], 1)
    backward = jnp.concatenate([medium_taps, zero], 1)
    return jnp.concatenate([forward, backward], 0)


def per_device(activations, norm_gain, in_proj, short_taps, medium_taps, cotangent):
    tok, own_width = activations.shape
    ch = in_proj.shape[2]
    act_full = lax.all_gather(activations, "tp", axis=1, tiled=True)
    gain_full = lax.all_gather(norm_gain, "tp", axis=0, tiled=True)
    width = act_full.shape[1]
    act_cols = lax.all_to_all(act_full, "seq", split_axis=1, concat_axis=0, tiled=True)
    act_float = act_full.astype(F32)
    inv_rms = lax.rsqrt(jnp.mean(act_float * act_float, axis=1, keepdims=True) + EPS)
    normed = (act_float * inv_rms * gain_full.astype(F32)).astype(BF16)
    weight = jnp.transpose(in_proj, (1, 0, 2))
    pre = jnp.einsum("td,jdc->jtc", normed, weight, preferred_element_type=F32).astype(BF16)
    vmem = pl.BlockSpec(memory_space=pltpu.VMEM)
    mix, gp = pl.pallas_call(
        mixer_kernel,
        out_shape=(
            jax.ShapeDtypeStruct((tok, ch), BF16),
            jax.ShapeDtypeStruct((3, tok, ch), BF16),
        ),
        in_specs=[vmem] * 4,
        out_specs=(vmem, vmem),
        scratch_shapes=mixer_scratch(tok, ch),
        compiler_params=pltpu.CompilerParams(
            collective_id=0, has_side_effects=True, vmem_limit_bytes=40 * 2**20
        ),
    )(pre, cotangent, short_taps, band_rows(medium_taps))
    stat = lax.psum(jnp.sum(gp.astype(F32) * pre.astype(F32), axis=(0, 2)), "tp")[:, None] / width
    sent = (gp.astype(F32) * inv_rms[None]).astype(BF16)
    gp_all = lax.all_gather(sent, "seq", axis=1, tiled=True)
    partial = jnp.einsum("jtc,jdc->td", gp, weight, preferred_element_type=F32).astype(BF16)
    grad_slice = lax.psum_scatter(partial, "tp", scatter_dimension=1, tiled=True).astype(F32)
    own_scaled = activations.astype(F32) * inv_rms
    grad_input = (inv_rms * (norm_gain.astype(F32) * grad_slice - own_scaled * stat)).astype(BF16)
    product = jnp.einsum("td,jtc->jdc", act_cols, gp_all, preferred_element_type=F32)
    share = width // lax.axis_size("seq")
    own_gain = lax.dynamic_slice_in_dim(gain_full, lax.axis_index("seq") * share, share, 0).astype(F32)
    grad_proj = (product * own_gain[None, :, None]).astype(BF16).transpose(1, 0, 2)
    return mix, grad_input, grad_proj


def solution(mesh):
    return jax.shard_map(
        per_device,
        mesh=mesh,
        in_specs=(
            P("seq", "tp"), P("tp"), P(None, None, "tp"), P(None, None, "tp"), P("tp", None), P("seq", "tp"),
        ),
        out_specs=(P("seq", "tp"), P("seq", "tp"), P("seq", None, "tp")),
        check_vma=False,
    )
```

```python
import functools

import jax
import jax.numpy as jnp
from jax import lax
from jax.experimental import pallas as pl
from jax.experimental.pallas import tpu as pltpu
from jax.sharding import PartitionSpec as P

GROUP = 16
LM = 128
BLK = 128
EPS = 1e-06
F32 = jnp.float32
BF16 = jnp.bfloat16
MESH = pl.DeviceIdType.MESH


def build_bands(rows_ref, band_ref):
    def one(g, carry):
        row = jnp.broadcast_to(rows_ref[pl.ds(g, 1), :], (BLK, 2 * BLK))
        band_ref[g] = pltpu.roll(row, 0, 1, stride=1, stride_axis=0).astype(BF16)
        return carry

    lax.fori_loop(0, rows_ref.shape[0], one, 0)


def apply_band(band_ref, first, source_ref, row0):
    lane = lax.broadcasted_iota(jnp.int32, (BLK, 128), 1) // GROUP
    halves = source_ref.shape[1] // 128

    def one(g, totals):
        new = []
        for h in range(halves):
            part = jnp.dot(
                band_ref[first + h * 8 + g],
                source_ref[row0 : row0 + 2 * BLK, h * 128 : h * 128 + 128],
                preferred_element_type=F32,
            )
            new.append(jnp.where(lane == g, part, totals[h]))
        return tuple(new)

    totals = lax.fori_loop(0, 8, one, tuple(jnp.zeros((BLK, 128), F32) for _ in range(halves)))
    return jnp.concatenate(totals, 1)


def mixer(pre, cot, taps, band, mix, gp, ext, feat, gext, gfext, gft, ptail, ghead, gtail, send, recv):
    tok, ch = pre.shape[1], pre.shape[2]
    n = lax.axis_size("seq")
    me = lax.axis_index("seq")
    after, before = lax.rem(me + 1, n), lax.rem(me + n - 1, n)
    first, last = me == 0, me == n - 1
    groups = ch // GROUP

    def remote(src, dst, index, to):
        return pltpu.make_async_remote_copy(
            src_ref=src, dst_ref=dst, send_sem=send.at[index], recv_sem=recv.at[index],
            device_id={"seq": to}, device_id_type=MESH,
        )

    tail_copy = remote(pre.at[:, pl.ds(tok - 16, 16), :], ptail, 0, after)
    tail_copy.start()
    for j in range(3):
        ext[j, 8 : 8 + tok, :] = pre[j].astype(F32)

    def short(j, lo, hi):
        total = taps[0, j : j + 1, :] * ext[j, 8 + lo : 8 + hi, :]
        total += taps[1, j : j + 1, :] * ext[j, 7 + lo : 7 + hi, :]
        total += taps[2, j : j + 1, :] * ext[j, 6 + lo : 6 + hi, :]
        return total.astype(BF16)

    def gate(lo, hi):
        k, v = short(1, lo, hi), short(2, lo, hi)
        feat[1, lo:hi, :] = k
        feat[2, lo:hi, :] = v
        gext[BLK + lo : BLK + hi, :] = (k.astype(F32) * v.astype(F32)).astype(BF16)

    gate(tok - BLK, tok)
    gated_copy = remote(gext.at[pl.ds(tok, BLK), :], gext.at[pl.ds(0, BLK), :], 1, after)
    gated_copy.start()

    tail_copy.wait_recv()
    for j in range(3):
        ext[j, 0:8, :] = jnp.where(first, 0.0, ptail[j].astype(F32)[8:16])
    q = short(0, 0, tok)
    feat[0] = q
    grad_out = cot[...].astype(F32)
    gfext[0:tok, :] = (grad_out * q.astype(F32)).astype(BF16)
    filt_copy = remote(gfext.at[pl.ds(0, BLK), :], gtail, 2, before)
    filt_copy.start()
    gate(0, tok - BLK)

    def grad_kv(lo):
        gg = apply_band(band, groups, gfext, lo)
        gft[1, lo : lo + BLK, :] = (gg * feat[2, lo : lo + BLK, :].astype(F32)).astype(BF16).astype(F32)
        gft[2, lo : lo + BLK, :] = (gg * feat[1, lo : lo + BLK, :].astype(F32)).astype(BF16).astype(F32)

    def forward(lo):
        filt = apply_band(band, 0, gext, lo)
        mix[lo : lo + BLK, :] = (feat[0, lo : lo + BLK, :].astype(F32) * filt).astype(BF16)
        gft[0, lo : lo + BLK, :] = (cot[lo : lo + BLK, :].astype(F32) * filt).astype(BF16).astype(F32)

    grad_kv(0)
    gated_copy.wait_recv()

    @pl.when(first)
    def _():
        gext[0:BLK, :] = jnp.zeros((BLK, ch), BF16)

    forward(0)
    for j in range(3):
        ghead[0, j] = gft[j, 0:16, :].astype(BF16)
    head_copy = remote(ghead.at[0], ghead.at[1], 3, before)
    head_copy.start()
    forward(BLK)
    filt_copy.wait_recv()
    gfext[tok : tok + BLK, :] = jnp.where(last, 0.0, gtail[...].astype(F32)).astype(BF16)
    grad_kv(BLK)
    head_copy.wait_recv()
    for j in range(3):
        gft[j, tok : tok + 8, :] = jnp.where(last, 0.0, ghead[1, j].astype(F32)[0:8])
    for j in range(3):
        total = taps[0, j : j + 1, :] * gft[j, 0:tok, :]
        total += taps[1, j : j + 1, :] * gft[j, 1 : tok + 1, :]
        total += taps[2, j : j + 1, :] * gft[j, 2 : tok + 2, :]
        gp[j] = total.astype(BF16)
    for copy in (tail_copy, gated_copy, filt_copy, head_copy):
        copy.wait_send()


def mixer_scratch(tok, ch):
    return [
        pltpu.VMEM((2 * ch // GROUP, BLK, 2 * BLK), BF16),
        pltpu.VMEM((3, tok + 8, ch), F32),
        pltpu.VMEM((3, tok, ch), BF16),
        pltpu.VMEM((tok + BLK, ch), BF16),
        pltpu.VMEM((tok + BLK, ch), BF16),
        pltpu.VMEM((3, tok + 8, ch), F32),
        pltpu.VMEM((3, 16, ch), BF16),
        pltpu.VMEM((2, 3, 16, ch), BF16),
        pltpu.VMEM((BLK, ch), BF16),
        pltpu.SemaphoreType.DMA((4,)),
        pltpu.SemaphoreType.DMA((4,)),
    ]


def whole_kernel(
    act, gain, weight, cot, taps, rows, mix, grad_in, grad_proj,
    ag, w, acc, ssq, inv, pre, gp, col, cols_t, gp_all, total, sib_out, sib_in, pair_out, pair_in, part, stats,
    load_sem, w_sem, ag_sem, fwd_sem, col_sem, colf_sem, gp_sem, sib_sem, pair_sem, stat_sem, statp_sem,
    band, *halo,
):
    n_seq, n_tp = lax.axis_size("seq"), lax.axis_size("tp")
    tok, own = act.shape
    ch = pre.shape[2]
    chips = n_tp // 2
    s, p = lax.axis_index("seq"), lax.axis_index("tp")
    q, core = p // 2, lax.rem(p, 2)
    sib = p + 1 - 2 * core
    width = n_tp * own

    def remote(src, dst, sems, index, to):
        return pltpu.make_async_remote_copy(
            src_ref=src, dst_ref=dst, send_sem=sems.at[0, index], recv_sem=sems.at[1, index],
            device_id=to, device_id_type=MESH,
        )

    def tp_peer(k):
        return lax.rem(q + k, chips) * 2 + core

    def tp_source(k):
        return lax.rem(q + chips - k, chips)

    def loop(lo, hi, body):
        def step(i, carry):
            body(i)
            return carry

        lax.fori_loop(lo, hi, step, 0)

    def block_rows(index):
        return pl.ds(pl.multiple_of(index * own, own), own)

    loads = (
        pltpu.make_async_copy(act, ag.at[p, pl.ds(0, tok), :], load_sem.at[0]),
        pltpu.make_async_copy(gain, ag.at[p, pl.ds(tok, 16), :], load_sem.at[1]),
    )
    for copy in loads:
        copy.start()

    def w_copy(index):
        return pltpu.make_async_copy(
            weight.at[:, block_rows(index), :], w.at[:, block_rows(index), :], w_sem.at[index]
        )

    loop(0, n_tp, lambda i: w_copy(lax.rem(p + i, n_tp)).start())

    barrier = pltpu.get_barrier_semaphore()

    def greet(k):
        pl.semaphore_signal(barrier, inc=1, device_id={"seq": s, "tp": tp_peer(k)}, device_id_type=MESH)
        to = lax.rem(s + k, n_seq)
        pl.semaphore_signal(barrier, inc=1, device_id={"seq": to, "tp": p}, device_id_type=MESH)

    loop(1, 8, greet)
    pl.semaphore_signal(barrier, inc=1, device_id={"seq": s, "tp": sib}, device_id_type=MESH)
    for copy in loads:
        copy.wait()
    pl.semaphore_wait(barrier, 15)

    def ag_copy(k):
        return remote(ag.at[p], ag.at[p], ag_sem, k, {"tp": tp_peer(k)})

    def ag_in(k):
        slot = tp_source(k) * 2 + core
        return remote(ag.at[slot], ag.at[slot], ag_sem, k, {"tp": sib})

    def fwd_copy(k):
        slot = tp_source(k) * 2 + core
        return remote(ag.at[slot], ag.at[slot], fwd_sem, k, {"tp": sib})

    def fwd_in(k):
        slot = tp_source(k) * 2 + 1 - core
        return remote(ag.at[slot], ag.at[slot], fwd_sem, k, {"tp": sib})

    def col_send(to):
        return pltpu.make_async_remote_copy(
            src_ref=ag.at[to * 2 + core, pl.ds(0, tok), :], dst_ref=col.at[s, core],
            send_sem=col_sem.at[0, to], recv_sem=col_sem.at[1, s],
            device_id={"seq": to}, device_id_type=MESH,
        )

    def col_in(source):
        return pltpu.make_async_remote_copy(
            src_ref=col.at[source, core], dst_ref=col.at[source, core],
            send_sem=col_sem.at[0, source], recv_sem=col_sem.at[1, source],
            device_id={"seq": source}, device_id_type=MESH,
        )

    loop(1, chips, lambda k: ag_copy(k).start())
    build_bands(rows, band)

    acc[...] = jnp.zeros_like(acc)
    ssq[...] = jnp.zeros_like(ssq)

    def absorb(slot):
        w_copy(slot).wait()
        x = ag[slot, 0:tok, :].astype(F32)
        g = ag[slot, tok : tok + 16, :].astype(F32)[0:1]
        square = x * x
        ssq[...] += sum(square[:, i * 128 : i * 128 + 128] for i in range(own // 128))
        scaled = (x * g).astype(BF16)
        for j in range(3):
            acc[j] += jnp.dot(scaled, w[j, block_rows(slot), :], preferred_element_type=F32)

    def gather(k):
        @pl.when(k > 0)
        def _():
            ag_in(k).wait_recv()

        source = tp_source(k)
        fwd_copy(k).start()

        @pl.when(source != s)
        def _():
            col_send(source).start()

        absorb(source * 2 + core)
        fwd_in(k).wait_recv()
        absorb(source * 2 + 1 - core)

    loop(0, chips, gather)

    inv[...] = jnp.broadcast_to(
        lax.rsqrt(jnp.sum(ssq[...], axis=1, keepdims=True) * (1.0 / width) + EPS), inv.shape
    )
    for j in range(3):
        pre[j] = (acc[j] * inv[:, 0:1]).astype(BF16)

    mixer(pre, cot, taps, band, mix, gp, *halo)

    def gp_copy(k):
        return remote(gp_all.at[s], gp_all.at[s], gp_sem, k, {"seq": lax.rem(s + k, n_seq)})

    def gp_in(k):
        slot = lax.rem(s + n_seq - k, n_seq)
        return remote(gp_all.at[slot], gp_all.at[slot], gp_sem, k, {"seq": slot})

    stat = jnp.zeros((tok, ch), F32)
    for j in range(3):
        value = gp[j].astype(F32)
        gp_all[s, j] = (value * inv[:, 0:1]).astype(BF16)
        stat += value * pre[j].astype(F32)
    loop(1, n_seq, lambda k: gp_copy(k).start())

    eye = lax.broadcasted_iota(jnp.int32, (128, 128), 0) == lax.broadcasted_iota(jnp.int32, (128, 128), 1)

    stat = jnp.sum(stat, axis=1, keepdims=True)
    stats[0] = jnp.zeros((8, 128), F32)
    for h in range(tok // 128):
        piece = jnp.where(eye, stat[h * 128 : h * 128 + 128], 0.0)
        stats[0, h : h + 1, :] = jnp.sum(piece, axis=0, keepdims=True)
    stat_sib = remote(stats.at[0], stats.at[1], statp_sem, 0, {"tp": sib})
    stat_sib.start()

    def partial(rows_):
        value = None
        for j in range(3):
            term = lax.dot_general(
                gp[j], w[j, rows_, :], (((1,), (1,)), ((), ())), preferred_element_type=F32
            )
            value = term if value is None else value + term
        return value

    def sib_copy(i):
        return remote(sib_out.at[i], sib_in.at[i], sib_sem, i, {"tp": sib})

    def pair_copy(i):
        return remote(pair_out.at[i], pair_in.at[i], pair_sem, i, {"tp": tp_peer(i + 1)})

    def finish(i):
        sib_copy(i).wait_recv()
        pair_out[i] = (part[lax.rem(i, 2)] + sib_in[i].astype(F32)).astype(BF16)
        pair_copy(i).start()

    def reduce(i):
        chip = lax.rem(q + 1 + i, chips)
        sib_out[i] = partial(block_rows(chip * 2 + 1 - core)).astype(BF16)
        sib_copy(i).start()
        part[lax.rem(i, 2)] = partial(block_rows(chip * 2 + core))

        @pl.when(i > 0)
        def _():
            finish(i - 1)

    loop(0, chips, reduce)

    stat_sib.wait_recv()
    stats[2] = stats[0] + stats[1]

    def stat_copy(k):
        return remote(stats.at[2], stats.at[2 + k], stat_sem, k, {"tp": tp_peer(k)})

    loop(1, chips, lambda k: stat_copy(k).start())

    def colf_copy(source):
        return remote(col.at[source, core], col.at[source, core], colf_sem, source, {"tp": sib})

    def colf_in(source):
        return remote(col.at[source, 1 - core], col.at[source, 1 - core], colf_sem, source, {"tp": sib})

    def seq_source(k):
        return lax.rem(s + n_seq - k, n_seq)

    def turn(source):
        for half in range(2):
            cols_t[source, half * own : half * own + own, :] = col[source, half].T

    def pass_on(k):
        col_in(seq_source(k)).wait_recv()
        colf_copy(seq_source(k)).start()

    for half in range(2):
        col[s, half] = ag[s * 2 + half, 0:tok, :]
    turn(s)
    loop(1, n_seq, pass_on)

    def turn_next(k):
        colf_in(seq_source(k)).wait_recv()
        turn(seq_source(k))

    loop(1, n_seq, turn_next)

    sib_copy(chips - 1).wait_recv()
    summed = part[(chips - 1) % 2] + sib_in[chips - 1].astype(F32)
    part[0] = summed

    def collect(k):
        pair_copy(k - 1).wait_recv()
        stat_copy(k).wait_recv()
        part[0] += pair_in[k - 1].astype(F32)

    loop(1, chips, collect)
    stat_rows = sum(stats[2 + k] for k in range(chips)) * (1.0 / width)
    own_gain = ag[p, tok : tok + 16, :].astype(F32)[0:1]
    for h in range(tok // 128):
        r = slice(h * 128, h * 128 + 128)
        stat_col = jnp.sum(jnp.where(eye, stat_rows[h : h + 1, :], 0.0), axis=1, keepdims=True)
        rms = inv[r, 0:1]
        scaled = ag[p, r, :].astype(F32) * rms
        grad_in[r, :] = (rms * (own_gain * part[0, r, :] - scaled * stat_col)).astype(BF16)

    total[...] = jnp.zeros_like(total)

    def product(k):
        @pl.when(k > 0)
        def _():
            gp_in(k).wait_recv()

        source = seq_source(k)

        def piece(c):
            r = pl.ds(pl.multiple_of(c * 128, 128), 128)
            left = cols_t[source, r, :]
            for j in range(3):
                total[j, r, :] += jnp.dot(left, gp_all[source, j], preferred_element_type=F32)

        loop(0, 2 * own // 128, piece)

    loop(0, n_seq, product)
    for c in range(2 * own // 128):
        lane = (c * 128) % own
        g = ag[s * 2 + c * 128 // own, tok : tok + 16, lane : lane + 128].astype(F32)[0:1]
        g_col = jnp.sum(jnp.where(eye, g, 0.0), axis=1, keepdims=True)
        for j in range(3):
            grad_proj[j, c * 128 : c * 128 + 128, :] = (total[j, c * 128 : c * 128 + 128, :] * g_col).astype(BF16)

    def settle(k):
        @pl.when(k > 0)
        def _():
            ag_copy(k).wait_send()
            gp_copy(k).wait_send()
            stat_copy(k).wait_send()
            pair_copy(k - 1).wait_send()

        fwd_copy(k).wait_send()
        sib_copy(k).wait_send()

        @pl.when(k != s)
        def _():
            col_send(k).wait_send()
            colf_copy(k).wait_send()

    loop(0, chips, settle)
    stat_sib.wait_send()


def band_rows(medium_taps):
    zero = jnp.zeros_like(medium_taps)
    forward = jnp.concatenate([zero[:, :1], medium_taps[:, ::-1], zero[:, 1:]], 1)
    backward = jnp.concatenate([medium_taps, zero], 1)
    return jnp.concatenate([forward, backward], 0)


def per_device(activations, norm_gain, in_proj, short_taps, medium_taps, cotangent):
    tok, own = activations.shape
    width, _, ch = in_proj.shape
    n_seq, n_tp = lax.axis_size("seq"), lax.axis_size("tp")
    chips = n_tp // 2
    vmem = pl.BlockSpec(memory_space=pltpu.VMEM)
    hbm = pl.BlockSpec(memory_space=pl.ANY)
    sems = lambda count: pltpu.SemaphoreType.DMA((2, count))
    mix, grad_in, grad_proj = pl.pallas_call(
        whole_kernel,
        out_shape=(
            jax.ShapeDtypeStruct((tok, ch), BF16),
            jax.ShapeDtypeStruct((tok, own), BF16),
            jax.ShapeDtypeStruct((3, 2 * own, ch), BF16),
        ),
        in_specs=[hbm] * 3 + [vmem] * 3,
        out_specs=(vmem,) * 3,
        scratch_shapes=[
            pltpu.VMEM((n_tp, tok + 16, own), BF16),
            pltpu.VMEM((3, width, ch), BF16),
            pltpu.VMEM((3, tok, ch), F32),
            pltpu.VMEM((tok, 128), F32),
            pltpu.VMEM((tok, 128), F32),
            pltpu.VMEM((3, tok, ch), BF16),
            pltpu.VMEM((3, tok, ch), BF16),
            pltpu.VMEM((n_seq, 2, tok, own), BF16),
            pltpu.VMEM((n_seq, 2 * own, tok), BF16),
            pltpu.VMEM((n_seq, 3, tok, ch), BF16),
            pltpu.VMEM((3, 2 * own, ch), F32),
            pltpu.VMEM((chips, tok, own), BF16),
            pltpu.VMEM((chips, tok, own), BF16),
            pltpu.VMEM((chips, tok, own), BF16),
            pltpu.VMEM((chips, tok, own), BF16),
            pltpu.VMEM((2, tok, own), F32),
            pltpu.VMEM((2 + chips, 8, 128), F32),
            pltpu.SemaphoreType.DMA((2,)),
            pltpu.SemaphoreType.DMA((n_tp,)),
            sems(chips), sems(chips), sems(n_seq), sems(n_seq), sems(n_seq), sems(chips), sems(chips), sems(chips), sems(1),
        ] + mixer_scratch(tok, ch),
        compiler_params=pltpu.CompilerParams(
            collective_id=0, has_side_effects=True, vmem_limit_bytes=60 * 2**20
        ),
    )(
        activations,
        jnp.broadcast_to(norm_gain[None], (16, own)),
        jnp.transpose(in_proj, (1, 0, 2)),
        cotangent,
        short_taps,
        band_rows(medium_taps),
    )
    return mix, grad_in, jnp.transpose(grad_proj, (1, 0, 2))


def solution(mesh):
    return jax.shard_map(
        per_device,
        mesh=mesh,
        in_specs=(
            P("seq", "tp"), P("tp"), P(None, None, "tp"), P(None, None, "tp"), P("tp", None), P("seq", "tp"),
        ),
        out_specs=(P("seq", "tp"), P("seq", "tp"), P("seq", None, "tp")),
        check_vma=False,
    )
```

```python
import jax
import jax.numpy as jnp
from jax import lax
from jax.experimental import pallas as pl
from jax.experimental.pallas import tpu as pltpu
from jax.sharding import PartitionSpec as P

GROUP = 16
LM = 128
BLK = 128
EPS = 1e-06
F32 = jnp.float32
BF16 = jnp.bfloat16
MESH = pl.DeviceIdType.MESH


def build_bands(taps_ref, band_ref):
    groups = taps_ref.shape[0]

    def one(g, carry):
        row = jnp.broadcast_to(taps_ref[pl.ds(g, 1), :], (BLK, LM))
        wide = jnp.concatenate([row, jnp.zeros((BLK, BLK), F32)], 1)
        wide = pltpu.roll(wide, 0, 1, stride=1, stride_axis=0)
        band_ref[groups + g] = wide.astype(BF16)
        band_ref[g, :, 0:BLK] = wide[:, BLK:].T.astype(BF16)
        band_ref[g, :, BLK:] = wide[:, 0:BLK].T.astype(BF16)
        return carry

    lax.fori_loop(0, groups, one, 0)


def apply_band(band_ref, first, source_ref, row0):
    lane = lax.broadcasted_iota(jnp.int32, (BLK, 128), 1) // GROUP
    halves = source_ref.shape[1] // 128

    def one(g, totals):
        new = []
        for h in range(halves):
            part = jnp.dot(
                band_ref[first + h * 8 + g],
                source_ref[row0 : row0 + 2 * BLK, h * 128 : h * 128 + 128],
                preferred_element_type=F32,
            )
            new.append(jnp.where(lane == g, part, totals[h]))
        return tuple(new)

    totals = lax.fori_loop(0, 8, one, tuple(jnp.zeros((BLK, 128), F32) for _ in range(halves)))
    return jnp.concatenate(totals, 1)


def mixer(pre, cot, taps, band, mix, gp, ext, feat, gext, gfext, gft, ptail, ghead, gtail, send, recv, hooks=()):
    tok, ch = pre.shape[1], pre.shape[2]
    n = lax.axis_size("seq")
    me = lax.axis_index("seq")
    after, before = lax.rem(me + 1, n), lax.rem(me + n - 1, n)
    first, last = me == 0, me == n - 1
    groups = ch // GROUP

    def remote(src, dst, index, to):
        return pltpu.make_async_remote_copy(
            src_ref=src, dst_ref=dst, send_sem=send.at[index], recv_sem=recv.at[index],
            device_id={"seq": to}, device_id_type=MESH,
        )

    tail_copy = remote(pre.at[:, pl.ds(tok - 16, 16), :], ptail, 0, after)
    tail_copy.start()
    for j in range(3):
        ext[j, 8 : 8 + tok, :] = pre[j].astype(F32)

    def short(j, lo, hi):
        total = taps[0, j : j + 1, :] * ext[j, 8 + lo : 8 + hi, :]
        total += taps[1, j : j + 1, :] * ext[j, 7 + lo : 7 + hi, :]
        total += taps[2, j : j + 1, :] * ext[j, 6 + lo : 6 + hi, :]
        return total.astype(BF16)

    def gate(lo, hi):
        k, v = short(1, lo, hi), short(2, lo, hi)
        feat[1, lo:hi, :] = k
        feat[2, lo:hi, :] = v
        gext[BLK + lo : BLK + hi, :] = (k.astype(F32) * v.astype(F32)).astype(BF16)

    gate(tok - BLK, tok)
    gated_copy = remote(gext.at[pl.ds(tok, BLK), :], gext.at[pl.ds(0, BLK), :], 1, after)
    gated_copy.start()

    hooks[0]()
    tail_copy.wait_recv()
    for j in range(3):
        ext[j, 0:8, :] = jnp.where(first, 0.0, ptail[j].astype(F32)[8:16])
    q = short(0, 0, tok)
    feat[0] = q
    grad_out = cot[...].astype(F32)
    gfext[0:tok, :] = (grad_out * q.astype(F32)).astype(BF16)
    filt_copy = remote(gfext.at[pl.ds(0, BLK), :], gtail, 2, before)
    filt_copy.start()
    gate(0, tok - BLK)

    def grad_kv(lo):
        gg = apply_band(band, groups, gfext, lo)
        gft[1, lo : lo + BLK, :] = (gg * feat[2, lo : lo + BLK, :].astype(F32)).astype(BF16).astype(F32)
        gft[2, lo : lo + BLK, :] = (gg * feat[1, lo : lo + BLK, :].astype(F32)).astype(BF16).astype(F32)

    def forward(lo):
        filt = apply_band(band, 0, gext, lo)
        mix[lo : lo + BLK, :] = (feat[0, lo : lo + BLK, :].astype(F32) * filt).astype(BF16)
        gft[0, lo : lo + BLK, :] = (cot[lo : lo + BLK, :].astype(F32) * filt).astype(BF16).astype(F32)

    grad_kv(0)
    hooks[1]()
    gated_copy.wait_recv()

    @pl.when(first)
    def _():
        gext[0:BLK, :] = jnp.zeros((BLK, ch), BF16)

    forward(0)
    for j in range(3):
        ghead[0, j] = gft[j, 0:16, :].astype(BF16)
    head_copy = remote(ghead.at[0], ghead.at[1], 3, before)
    head_copy.start()
    forward(BLK)
    hooks[2]()
    filt_copy.wait_recv()
    gfext[tok : tok + BLK, :] = jnp.where(last, 0.0, gtail[...].astype(F32)).astype(BF16)
    grad_kv(BLK)
    head_copy.wait_recv()
    for j in range(3):
        gft[j, tok : tok + 8, :] = jnp.where(last, 0.0, ghead[1, j].astype(F32)[0:8])
    for j in range(3):
        total = taps[0, j : j + 1, :] * gft[j, 0:tok, :]
        total += taps[1, j : j + 1, :] * gft[j, 1 : tok + 1, :]
        total += taps[2, j : j + 1, :] * gft[j, 2 : tok + 2, :]
        gp[j] = total.astype(BF16)
    for copy in (tail_copy, gated_copy, filt_copy, head_copy):
        copy.wait_send()


def mixer_scratch(tok, ch):
    return [
        pltpu.VMEM((2 * ch // GROUP, BLK, 2 * BLK), BF16),
        pltpu.VMEM((3, tok + 8, ch), F32),
        pltpu.VMEM((3, tok, ch), BF16),
        pltpu.VMEM((tok + BLK, ch), BF16),
        pltpu.VMEM((tok + BLK, ch), BF16),
        pltpu.VMEM((3, tok + 8, ch), F32),
        pltpu.VMEM((3, 16, ch), BF16),
        pltpu.VMEM((2, 3, 16, ch), BF16),
        pltpu.VMEM((BLK, ch), BF16),
        pltpu.SemaphoreType.DMA((4,)),
        pltpu.SemaphoreType.DMA((4,)),
    ]


class Gather:
    def __init__(self, ring, pair, block, slot, device, send, recv):
        self.ring, self.pair, self.block, self.slot, self.device = ring, pair, block, slot, device
        self.send, self.recv = send, recv

    def at(self, step, flip):
        ring = lax.rem(self.ring + step + 4, 4)
        return ring, (1 - self.pair if flip else self.pair)

    def source(self, i):
        where = ((0, 1), (-1, 0), (1, 0), (-1, 1), (1, 1), (2, 0), (2, 1))[i]
        return self.slot(*self.at(*where))

    def copy(self, i):
        what, to = (
            ((0, 0), (0, 1)), ((0, 0), (1, 0)), ((0, 0), (-1, 0)), ((0, 1), (1, 0)),
            ((0, 1), (-1, 0)), ((-1, 0), (1, 0)), ((1, 1), (-1, 0)),
        )[i]
        block = self.block(self.slot(*self.at(*what)))
        return pltpu.make_async_remote_copy(
            src_ref=block, dst_ref=block, send_sem=self.send.at[i], recv_sem=self.recv.at[i],
            device_id=self.device(*self.at(*to)), device_id_type=MESH,
        )

    def start(self):
        for i in (1, 2, 0):
            self.copy(i).start()

    def arrive(self, i):
        block = self.block(self.source(i))
        pltpu.make_async_remote_copy(
            src_ref=block, dst_ref=block, send_sem=self.send.at[i], recv_sem=self.recv.at[i],
            device_id=self.device(*self.at(0, 1)), device_id_type=MESH,
        ).wait_recv()
        for following in {0: (3, 4), 1: (5,), 4: (6,)}.get(i, ()):
            self.copy(following).start()
        return self.source(i)

    def settle(self):
        for i in range(7):
            self.copy(i).wait_send()


def whole_kernel(
    act, gain, weight, cot, taps, medium, mix, grad_in, grad_proj,
    ag, w, acc, ssq, inv, pre, gp, col, cols_t, gp_all, total, sib_out, sib_in, pair_out, pair_in, part, stats,
    load_sem, w_sem, ag_sem, fwd_sem, turn_sem, col_sem, colf_sem, gp_sem, sib_sem, pair_sem, stat_sem, statp_sem,
    band, *halo,
):
    n_seq, n_tp = lax.axis_size("seq"), lax.axis_size("tp")
    tok, own = act.shape
    ch = pre.shape[2]
    chips = n_tp // 2
    s, p = lax.axis_index("seq"), lax.axis_index("tp")
    q, core = p // 2, lax.rem(p, 2)
    sib = p + 1 - 2 * core
    width = n_tp * own

    def remote(src, dst, sems, index, to):
        return pltpu.make_async_remote_copy(
            src_ref=src, dst_ref=dst, send_sem=sems.at[0, index], recv_sem=sems.at[1, index],
            device_id=to, device_id_type=MESH,
        )

    def tp_peer(k):
        return lax.rem(q + k, chips) * 2 + core

    def loop(lo, hi, body):
        def step(i, carry):
            body(i)
            return carry

        lax.fori_loop(lo, hi, step, 0)

    def block_rows(index):
        return pl.ds(pl.multiple_of(index * own, own), own)

    loads = (
        pltpu.make_async_copy(act, ag.at[p, pl.ds(0, tok), :], load_sem.at[0]),
        pltpu.make_async_copy(gain, ag.at[p, pl.ds(tok, 16), :], load_sem.at[1]),
    )
    for copy in loads:
        copy.start()

    def w_copy(index):
        return pltpu.make_async_copy(
            weight.at[:, block_rows(index), :], w.at[:, block_rows(index), :], w_sem.at[index]
        )

    loop(0, n_tp, lambda i: w_copy(lax.rem(p + i, n_tp)).start())

    barrier = pltpu.get_barrier_semaphore()

    def greet(k):
        pl.semaphore_signal(barrier, inc=1, device_id={"seq": s, "tp": tp_peer(k)}, device_id_type=MESH)
        to = lax.rem(s + k, n_seq)
        pl.semaphore_signal(barrier, inc=1, device_id={"seq": to, "tp": p}, device_id_type=MESH)

    loop(1, 8, greet)
    pl.semaphore_signal(barrier, inc=1, device_id={"seq": s, "tp": sib}, device_id_type=MESH)

    @pl.when(q != s)
    def _():
        pl.semaphore_signal(barrier, inc=1, device_id={"seq": q, "tp": 2 * s + core}, device_id_type=MESH)

    for copy in loads:
        copy.wait()
    pl.semaphore_wait(barrier, 15 + jnp.where(q != s, 1, 0))

    y, z_lo = q // 2, lax.rem(q, 2)
    gather = Gather(
        y, z_lo, lambda chip: ag.at[chip * 2 + core], lambda r, z: r * 2 + z,
        lambda r, z: {"tp": (r * 2 + z) * 2 + core}, ag_sem.at[0], ag_sem.at[1],
    )
    gather.start()

    def turned_copy():
        return pltpu.make_async_remote_copy(
            src_ref=ag.at[p, pl.ds(0, tok), :], dst_ref=col.at[s, core],
            send_sem=turn_sem.at[0], recv_sem=turn_sem.at[1],
            device_id={"seq": q, "tp": 2 * s + core}, device_id_type=MESH,
        )

    @pl.when(q != s)
    def _():
        turned_copy().start()

    @pl.when(q == s)
    def _():
        col[s, core] = ag[p, 0:tok, :]

    columns = Gather(
        y, z_lo, lambda chip: col.at[chip, core], lambda r, z: r * 2 + z,
        lambda r, z: {"tp": (r * 2 + z) * 2 + core}, col_sem.at[0], col_sem.at[1],
    )

    def fwd_copy(i, chip):
        slot = chip * 2 + core
        return remote(ag.at[slot], ag.at[slot], fwd_sem, i, {"tp": sib})

    def fwd_in(i, chip):
        slot = chip * 2 + 1 - core
        return remote(ag.at[slot], ag.at[slot], fwd_sem, i, {"tp": sib})

    def colf_copy(i, chip):
        return remote(col.at[chip, core], col.at[chip, core], colf_sem, i, {"tp": sib})

    def colf_in(i, chip):
        return remote(col.at[chip, 1 - core], col.at[chip, 1 - core], colf_sem, i, {"tp": sib})

    fwd_copy(7, q).start()
    build_bands(medium, band)
    acc[...] = jnp.zeros_like(acc)
    ssq[...] = jnp.zeros_like(ssq)

    def absorb(slot):
        w_copy(slot).wait()
        x = ag[slot, 0:tok, :].astype(F32)
        g = ag[slot, tok : tok + 16, :].astype(F32)[0:1]
        square = x * x
        ssq[...] += sum(square[:, i * 128 : i * 128 + 128] for i in range(own // 128))
        scaled = (x * g).astype(BF16)
        for j in range(3):
            acc[j] += jnp.dot(scaled, w[j, block_rows(slot), :], preferred_element_type=F32)

    def absorb_both(i, chip):
        absorb(chip * 2 + core)
        fwd_in(i, chip).wait_recv()
        absorb(chip * 2 + 1 - core)

    def take(i):
        chip = gather.arrive(i)
        fwd_copy(i, chip).start()
        return chip

    def pass_on(i):
        colf_copy(i, columns.arrive(i)).start()

    absorb_both(7, q)
    for i in (1, 2, 0, 4, 3):
        absorb_both(i, take(i))

    @pl.when(q != s)
    def _():
        turned_copy().wait_recv()

    columns.start()
    colf_copy(7, q).start()
    five = take(5)
    six = take(6)
    absorb_both(5, five)
    absorb_both(6, six)

    inv[...] = jnp.broadcast_to(
        lax.rsqrt(jnp.sum(ssq[...], axis=1, keepdims=True) * (1.0 / width) + EPS), inv.shape
    )
    for j in range(3):
        pre[j] = (acc[j] * inv[:, 0:1]).astype(BF16)

    mixer(
        pre, cot, taps, band, mix, gp, *halo,
        hooks=(
            lambda: (pass_on(1), pass_on(2)),
            lambda: pass_on(0),
            lambda: (pass_on(4), pass_on(3)),
        ),
    )

    seq_gather = Gather(
        lax.rem(s, 4), s // 4, lambda slot: gp_all.at[slot], lambda r, z: z * 4 + r,
        lambda r, z: {"seq": z * 4 + r}, gp_sem.at[0], gp_sem.at[1],
    )
    stat = jnp.zeros((tok, ch), F32)
    for j in range(3):
        value = gp[j].astype(F32)
        gp_all[s, j] = (value * inv[:, 0:1]).astype(BF16)
        stat += value * pre[j].astype(F32)
    seq_gather.start()

    eye = lax.broadcasted_iota(jnp.int32, (128, 128), 0) == lax.broadcasted_iota(jnp.int32, (128, 128), 1)

    stat = jnp.sum(stat, axis=1, keepdims=True)
    stats[0] = jnp.zeros((8, 128), F32)
    for h in range(tok // 128):
        piece = jnp.where(eye, stat[h * 128 : h * 128 + 128], 0.0)
        stats[0, h : h + 1, :] = jnp.sum(piece, axis=0, keepdims=True)
    stat_sib = remote(stats.at[0], stats.at[1], statp_sem, 0, {"tp": sib})
    stat_sib.start()

    def partial(rows_):
        value = None
        for j in range(3):
            term = lax.dot_general(
                gp[j], w[j, rows_, :], (((1,), (1,)), ((), ())), preferred_element_type=F32
            )
            value = term if value is None else value + term
        return value

    def sib_copy(i):
        return remote(sib_out.at[i], sib_in.at[i], sib_sem, i, {"tp": sib})

    def pair_copy(i):
        return remote(pair_out.at[i], pair_in.at[i], pair_sem, i, {"tp": tp_peer(i + 1)})

    def finish(i):
        sib_copy(i).wait_recv()
        pair_out[i] = (part[lax.rem(i, 2)] + sib_in[i].astype(F32)).astype(BF16)
        pair_copy(i).start()

    def reduce(i):
        chip = lax.rem(q + 1 + i, chips)
        sib_out[i] = partial(block_rows(chip * 2 + 1 - core)).astype(BF16)
        sib_copy(i).start()
        part[lax.rem(i, 2)] = partial(block_rows(chip * 2 + core))

        @pl.when(i > 0)
        def _():
            finish(i - 1)

    loop(0, chips, reduce)

    stat_sib.wait_recv()
    stats[2] = stats[0] + stats[1]

    def stat_copy(k):
        return remote(stats.at[2], stats.at[2 + k], stat_sem, k, {"tp": tp_peer(k)})

    loop(1, chips, lambda k: stat_copy(k).start())

    def turn(chip):
        for half in range(2):
            cols_t[chip, half * own : half * own + own, :] = col[chip, half].T

    def turn_in(i, chip):
        colf_in(i, chip).wait_recv()
        turn(chip)

    def product(source, begin=False):
        for j in range(3):
            term = jnp.dot(cols_t[source], gp_all[source, j], preferred_element_type=F32)
            total[j] = term if begin else total[j] + term

    pass_on(5)
    pass_on(6)
    turn_in(7, q)
    for i in range(7):
        turn_in(i, columns.source(i))
    product(s, True)
    for i in (1, 2, 0, 4, 3):
        product(seq_gather.arrive(i))

    sib_copy(chips - 1).wait_recv()
    summed = part[(chips - 1) % 2] + sib_in[chips - 1].astype(F32)
    part[0] = summed

    def collect(k):
        pair_copy(k - 1).wait_recv()
        stat_copy(k).wait_recv()
        part[0] += pair_in[k - 1].astype(F32)

    loop(1, chips, collect)
    stat_rows = sum(stats[2 + k] for k in range(chips)) * (1.0 / width)
    own_gain = ag[p, tok : tok + 16, :].astype(F32)[0:1]
    for h in range(tok // 128):
        r = slice(h * 128, h * 128 + 128)
        stat_col = jnp.sum(jnp.where(eye, stat_rows[h : h + 1, :], 0.0), axis=1, keepdims=True)
        rms = inv[r, 0:1]
        scaled = ag[p, r, :].astype(F32) * rms
        grad_in[r, :] = (rms * (own_gain * part[0, r, :] - scaled * stat_col)).astype(BF16)

    for i in (5, 6):
        product(seq_gather.arrive(i))
    for c in range(2 * own // 128):
        lane = (c * 128) % own
        g = ag[s * 2 + c * 128 // own, tok : tok + 16, lane : lane + 128].astype(F32)[0:1]
        g_col = jnp.sum(jnp.where(eye, g, 0.0), axis=1, keepdims=True)
        for j in range(3):
            grad_proj[j, c * 128 : c * 128 + 128, :] = (total[j, c * 128 : c * 128 + 128, :] * g_col).astype(BF16)

    def settle(k):
        @pl.when(k > 0)
        def _():
            stat_copy(k).wait_send()
            pair_copy(k - 1).wait_send()

        sib_copy(k).wait_send()

    loop(0, chips, settle)
    for group in (gather, columns, seq_gather):
        group.settle()
    for i in range(8):
        chip = q if i == 7 else gather.source(i)
        fwd_copy(i, chip).wait_send()
        colf_copy(i, chip).wait_send()

    @pl.when(q != s)
    def _():
        turned_copy().wait_send()

    stat_sib.wait_send()


def per_device(activations, norm_gain, in_proj, short_taps, medium_taps, cotangent):
    tok, own = activations.shape
    width, _, ch = in_proj.shape
    n_seq, n_tp = lax.axis_size("seq"), lax.axis_size("tp")
    chips = n_tp // 2
    vmem = pl.BlockSpec(memory_space=pltpu.VMEM)
    hbm = pl.BlockSpec(memory_space=pl.ANY)
    sems = lambda count: pltpu.SemaphoreType.DMA((2, count))
    mix, grad_in, grad_proj = pl.pallas_call(
        whole_kernel,
        out_shape=(
            jax.ShapeDtypeStruct((tok, ch), BF16),
            jax.ShapeDtypeStruct((tok, own), BF16),
            jax.ShapeDtypeStruct((3, 2 * own, ch), BF16),
        ),
        in_specs=[hbm] * 3 + [vmem] * 3,
        out_specs=(vmem,) * 3,
        scratch_shapes=[
            pltpu.VMEM((n_tp, tok + 16, own), BF16),
            pltpu.VMEM((3, width, ch), BF16),
            pltpu.VMEM((3, tok, ch), F32),
            pltpu.VMEM((tok, 128), F32),
            pltpu.VMEM((tok, 128), F32),
            pltpu.VMEM((3, tok, ch), BF16),
            pltpu.VMEM((3, tok, ch), BF16),
            pltpu.VMEM((n_seq, 2, tok, own), BF16),
            pltpu.VMEM((n_seq, 2 * own, tok), BF16),
            pltpu.VMEM((n_seq, 3, tok, ch), BF16),
            pltpu.VMEM((3, 2 * own, ch), F32),
            pltpu.VMEM((chips, tok, own), BF16),
            pltpu.VMEM((chips, tok, own), BF16),
            pltpu.VMEM((chips, tok, own), BF16),
            pltpu.VMEM((chips, tok, own), BF16),
            pltpu.VMEM((2, tok, own), F32),
            pltpu.VMEM((2 + chips, 8, 128), F32),
            pltpu.SemaphoreType.DMA((2,)),
            pltpu.SemaphoreType.DMA((n_tp,)),
            sems(7), sems(8), pltpu.SemaphoreType.DMA((2,)), sems(7), sems(8), sems(7), sems(chips), sems(chips), sems(chips), sems(1),
        ] + mixer_scratch(tok, ch),
        compiler_params=pltpu.CompilerParams(
            collective_id=0, has_side_effects=True, vmem_limit_bytes=60 * 2**20
        ),
    )(
        activations,
        jnp.broadcast_to(norm_gain[None], (16, own)),
        jnp.transpose(in_proj, (1, 0, 2)),
        cotangent,
        short_taps,
        medium_taps,
    )
    return mix, grad_in, jnp.transpose(grad_proj, (1, 0, 2))


def solution(mesh):
    return jax.shard_map(
        per_device,
        mesh=mesh,
        in_specs=(
            P("seq", "tp"), P("tp"), P(None, None, "tp"), P(None, None, "tp"), P("tp", None), P("seq", "tp"),
        ),
        out_specs=(P("seq", "tp"), P("seq", "tp"), P("seq", None, "tp")),
        check_vma=False,
    )
```

```python
import jax
import jax.numpy as jnp
from jax import lax
from jax.experimental import pallas as pl
from jax.experimental.pallas import tpu as pltpu
from jax.sharding import PartitionSpec as P

GROUP = 16
LM = 128
BLK = 128
EPS = 1e-06
F32 = jnp.float32
BF16 = jnp.bfloat16
MESH = pl.DeviceIdType.MESH


def build_bands(taps_ref, band_ref):
    groups = taps_ref.shape[0]

    def one(g, carry):
        row = jnp.broadcast_to(taps_ref[pl.ds(g, 1), :], (BLK, LM))
        wide = jnp.concatenate([row, jnp.zeros((BLK, BLK), F32)], 1)
        wide = pltpu.roll(wide, 0, 1, stride=1, stride_axis=0)
        band_ref[groups + g] = wide.astype(BF16)
        band_ref[g, :, 0:BLK] = wide[:, BLK:].T.astype(BF16)
        band_ref[g, :, BLK:] = wide[:, 0:BLK].T.astype(BF16)
        return carry

    lax.fori_loop(0, groups, one, 0)


def apply_band(band_ref, first, source_ref, row0):
    lane = lax.broadcasted_iota(jnp.int32, (BLK, 128), 1) // GROUP
    halves = source_ref.shape[1] // 128

    def one(g, totals):
        new = []
        for h in range(halves):
            part = jnp.dot(
                band_ref[first + h * 8 + g],
                source_ref[row0 : row0 + 2 * BLK, h * 128 : h * 128 + 128],
                preferred_element_type=F32,
            )
            new.append(jnp.where(lane == g, part, totals[h]))
        return tuple(new)

    totals = lax.fori_loop(0, 8, one, tuple(jnp.zeros((BLK, 128), F32) for _ in range(halves)))
    return jnp.concatenate(totals, 1)


def mixer(pre, cot, taps, band, mix, gp, ext, feat, gext, gfext, gft, ptail, ghead, gtail, send, recv):
    tok, ch = pre.shape[1], pre.shape[2]
    n = lax.axis_size("seq")
    me = lax.axis_index("seq")
    after, before = lax.rem(me + 1, n), lax.rem(me + n - 1, n)
    first, last = me == 0, me == n - 1
    groups = ch // GROUP

    def remote(src, dst, index, to):
        return pltpu.make_async_remote_copy(
            src_ref=src, dst_ref=dst, send_sem=send.at[index], recv_sem=recv.at[index],
            device_id={"seq": to}, device_id_type=MESH,
        )

    tail_copy = remote(pre.at[:, pl.ds(tok - 16, 16), :], ptail, 0, after)
    tail_copy.start()
    for j in range(3):
        ext[j, 8 : 8 + tok, :] = pre[j].astype(F32)

    def short(j, lo, hi):
        total = taps[0, j : j + 1, :] * ext[j, 8 + lo : 8 + hi, :]
        total += taps[1, j : j + 1, :] * ext[j, 7 + lo : 7 + hi, :]
        total += taps[2, j : j + 1, :] * ext[j, 6 + lo : 6 + hi, :]
        return total.astype(BF16)

    def gate(lo, hi):
        k, v = short(1, lo, hi), short(2, lo, hi)
        feat[1, lo:hi, :] = k
        feat[2, lo:hi, :] = v
        gext[BLK + lo : BLK + hi, :] = (k.astype(F32) * v.astype(F32)).astype(BF16)

    gate(tok - BLK, tok)
    gated_copy = remote(gext.at[pl.ds(tok, BLK), :], gext.at[pl.ds(0, BLK), :], 1, after)
    gated_copy.start()

    tail_copy.wait_recv()
    for j in range(3):
        ext[j, 0:8, :] = jnp.where(first, 0.0, ptail[j].astype(F32)[8:16])
    q = short(0, 0, tok)
    feat[0] = q
    grad_out = cot[...].astype(F32)
    gfext[0:tok, :] = (grad_out * q.astype(F32)).astype(BF16)
    filt_copy = remote(gfext.at[pl.ds(0, BLK), :], gtail, 2, before)
    filt_copy.start()
    gate(0, tok - BLK)

    def grad_kv(lo):
        gg = apply_band(band, groups, gfext, lo)
        gft[1, lo : lo + BLK, :] = (gg * feat[2, lo : lo + BLK, :].astype(F32)).astype(BF16).astype(F32)
        gft[2, lo : lo + BLK, :] = (gg * feat[1, lo : lo + BLK, :].astype(F32)).astype(BF16).astype(F32)

    def forward(lo):
        filt = apply_band(band, 0, gext, lo)
        mix[lo : lo + BLK, :] = (feat[0, lo : lo + BLK, :].astype(F32) * filt).astype(BF16)
        gft[0, lo : lo + BLK, :] = (cot[lo : lo + BLK, :].astype(F32) * filt).astype(BF16).astype(F32)

    grad_kv(0)
    gated_copy.wait_recv()

    @pl.when(first)
    def _():
        gext[0:BLK, :] = jnp.zeros((BLK, ch), BF16)

    forward(0)
    for j in range(3):
        ghead[0, j] = gft[j, 0:16, :].astype(BF16)
    head_copy = remote(ghead.at[0], ghead.at[1], 3, before)
    head_copy.start()
    forward(BLK)
    filt_copy.wait_recv()
    gfext[tok : tok + BLK, :] = jnp.where(last, 0.0, gtail[...].astype(F32)).astype(BF16)
    grad_kv(BLK)
    head_copy.wait_recv()
    for j in range(3):
        gft[j, tok : tok + 8, :] = jnp.where(last, 0.0, ghead[1, j].astype(F32)[0:8])
    for j in range(3):
        total = taps[0, j : j + 1, :] * gft[j, 0:tok, :]
        total += taps[1, j : j + 1, :] * gft[j, 1 : tok + 1, :]
        total += taps[2, j : j + 1, :] * gft[j, 2 : tok + 2, :]
        gp[j] = total.astype(BF16)
    for copy in (tail_copy, gated_copy, filt_copy, head_copy):
        copy.wait_send()


def mixer_scratch(tok, ch):
    return [
        pltpu.VMEM((2 * ch // GROUP, BLK, 2 * BLK), BF16),
        pltpu.VMEM((3, tok + 8, ch), F32),
        pltpu.VMEM((3, tok, ch), BF16),
        pltpu.VMEM((tok + BLK, ch), BF16),
        pltpu.VMEM((tok + BLK, ch), BF16),
        pltpu.VMEM((3, tok + 8, ch), F32),
        pltpu.VMEM((3, 16, ch), BF16),
        pltpu.VMEM((2, 3, 16, ch), BF16),
        pltpu.VMEM((BLK, ch), BF16),
        pltpu.SemaphoreType.DMA((4,)),
        pltpu.SemaphoreType.DMA((4,)),
    ]


class Gather:
    def __init__(self, ring, pair, block, slot, device, send, recv):
        self.ring, self.pair, self.block, self.slot, self.device = ring, pair, block, slot, device
        self.send, self.recv = send, recv

    def at(self, step, flip):
        ring = lax.rem(self.ring + step + 4, 4)
        return ring, (1 - self.pair if flip else self.pair)

    def source(self, i):
        where = ((0, 1), (-1, 0), (1, 0), (-1, 1), (1, 1), (2, 0), (2, 1))[i]
        return self.slot(*self.at(*where))

    def copy(self, i):
        what, to = (
            ((0, 0), (0, 1)), ((0, 0), (1, 0)), ((0, 0), (-1, 0)), ((0, 1), (1, 0)),
            ((0, 1), (-1, 0)), ((-1, 0), (1, 0)), ((1, 1), (-1, 0)),
        )[i]
        block = self.block(self.slot(*self.at(*what)))
        return pltpu.make_async_remote_copy(
            src_ref=block, dst_ref=block, send_sem=self.send.at[i], recv_sem=self.recv.at[i],
            device_id=self.device(*self.at(*to)), device_id_type=MESH,
        )

    def start(self):
        for i in (1, 2, 0):
            self.copy(i).start()

    def arrive(self, i):
        block = self.block(self.source(i))
        pltpu.make_async_remote_copy(
            src_ref=block, dst_ref=block, send_sem=self.send.at[i], recv_sem=self.recv.at[i],
            device_id=self.device(*self.at(0, 1)), device_id_type=MESH,
        ).wait_recv()
        for following in {0: (3, 4), 1: (5,), 4: (6,)}.get(i, ()):
            self.copy(following).start()
        return self.source(i)

    def settle(self):
        for i in range(7):
            self.copy(i).wait_send()


def whole_kernel(
    act, gain, weight, cot, taps, medium, mix, grad_in, grad_proj,
    ag, w, acc, ssq, inv, pre, gp, col, cols_t, gp_all, total, sib_out, sib_in, pair_out, pair_in, part, kept, stats,
    load_sem, w_sem, ag_sem, fwd_sem, col_sem, spread_sem, colf_sem, gp_sem, sib_sem, pair_sem, stat_sem, statp_sem,
    band, *halo,
):
    n_seq, n_tp = lax.axis_size("seq"), lax.axis_size("tp")
    tok, own = act.shape
    ch = pre.shape[2]
    chips = n_tp // 2
    s, p = lax.axis_index("seq"), lax.axis_index("tp")
    q, core = p // 2, lax.rem(p, 2)
    sib = p + 1 - 2 * core
    width = n_tp * own

    def remote(src, dst, sems, index, to):
        return pltpu.make_async_remote_copy(
            src_ref=src, dst_ref=dst, send_sem=sems.at[0, index], recv_sem=sems.at[1, index],
            device_id=to, device_id_type=MESH,
        )

    def tp_peer(k):
        return lax.rem(q + k, chips) * 2 + core

    def loop(lo, hi, body):
        def step(i, carry):
            body(i)
            return carry

        lax.fori_loop(lo, hi, step, 0)

    def block_rows(index):
        return pl.ds(pl.multiple_of(index * own, own), own)

    loads = (
        pltpu.make_async_copy(act, ag.at[p, pl.ds(0, tok), :], load_sem.at[0]),
        pltpu.make_async_copy(gain, ag.at[p, pl.ds(tok, 16), :], load_sem.at[1]),
    )
    for copy in loads:
        copy.start()

    def w_copy(index):
        return pltpu.make_async_copy(
            weight.at[:, block_rows(index), :], w.at[:, block_rows(index), :], w_sem.at[index]
        )

    loop(0, n_tp, lambda i: w_copy(lax.rem(p + i, n_tp)).start())

    barrier = pltpu.get_barrier_semaphore()

    def greet(k):
        pl.semaphore_signal(barrier, inc=1, device_id={"seq": s, "tp": tp_peer(k)}, device_id_type=MESH)
        to = lax.rem(s + k, n_seq)
        pl.semaphore_signal(barrier, inc=1, device_id={"seq": to, "tp": p}, device_id_type=MESH)

    loop(1, 8, greet)
    pl.semaphore_signal(barrier, inc=1, device_id={"seq": s, "tp": sib}, device_id_type=MESH)

    for copy in loads:
        copy.wait()
    pl.semaphore_wait(barrier, 15)

    y, z_lo = q // 2, lax.rem(q, 2)
    gather = Gather(
        y, z_lo, lambda chip: ag.at[chip * 2 + core], lambda r, z: r * 2 + z,
        lambda r, z: {"tp": (r * 2 + z) * 2 + core}, ag_sem.at[0], ag_sem.at[1],
    )
    gather.start()

    z_hi, x_at = s // 4, lax.rem(s, 4)
    def col_send(to):
        return pltpu.make_async_remote_copy(
            src_ref=ag.at[to * 2 + core, pl.ds(0, tok), :], dst_ref=col.at[s, core],
            send_sem=col_sem.at[0, to], recv_sem=col_sem.at[1, s],
            device_id={"seq": to}, device_id_type=MESH,
        )

    def col_in(source):
        return pltpu.make_async_remote_copy(
            src_ref=col.at[source, core], dst_ref=col.at[source, core],
            send_sem=col_sem.at[0, source], recv_sem=col_sem.at[1, source],
            device_id={"seq": source}, device_id_type=MESH,
        )

    def col_due(chip):
        near = chip // 4 == z_hi
        return (near & (lax.rem(chip, 4) != x_at)) | (~near & (lax.rem(chip + y, 4) == x_at))

    def col_start(chip):
        @pl.when(col_due(chip))
        def _():
            col_send(chip).start()

    def fetched(step):
        return (1 - z_hi) * 4 + lax.rem(x_at + y + step + 4, 4)

    def spread(i):
        step, part_rows, to = (
            (0, pl.ds(0, tok), 1), (0, pl.ds(0, tok), 3), (-1, pl.ds(0, tok // 2), 1), (1, pl.ds(tok // 2, tok // 2), 3),
        )[i]
        block = col.at[fetched(step), core, part_rows, :]
        return remote(block, block, spread_sem, i, {"tp": (lax.rem(y + to, 4) * 2 + z_lo) * 2 + core})

    def spread_in(i):
        step, part_rows = (
            (-1, pl.ds(0, tok)), (1, pl.ds(0, tok)), (2, pl.ds(0, tok // 2)), (2, pl.ds(tok // 2, tok // 2)),
        )[i]
        block = col.at[fetched(step), core, part_rows, :]
        return remote(block, block, spread_sem, i, {"tp": sib})

    def fwd_copy(i, chip):
        slot = chip * 2 + core
        return remote(ag.at[slot], ag.at[slot], fwd_sem, i, {"tp": sib})

    def fwd_in(i, chip):
        slot = chip * 2 + 1 - core
        return remote(ag.at[slot], ag.at[slot], fwd_sem, i, {"tp": sib})

    def colf_copy(source):
        return remote(col.at[source, core], col.at[source, core], colf_sem, source, {"tp": sib})

    def colf_in(source):
        return remote(col.at[source, 1 - core], col.at[source, 1 - core], colf_sem, source, {"tp": sib})

    col_start(q)
    fwd_copy(7, q).start()
    build_bands(medium, band)
    acc[...] = jnp.zeros_like(acc)
    ssq[...] = jnp.zeros_like(ssq)

    def absorb(slot):
        w_copy(slot).wait()
        x = ag[slot, 0:tok, :].astype(F32)
        g = ag[slot, tok : tok + 16, :].astype(F32)[0:1]
        square = x * x
        ssq[...] += sum(square[:, i * 128 : i * 128 + 128] for i in range(own // 128))
        scaled = (x * g).astype(BF16)
        for j in range(3):
            acc[j] += jnp.dot(scaled, w[j, block_rows(slot), :], preferred_element_type=F32)

    def absorb_both(i, chip):
        absorb(chip * 2 + core)
        fwd_in(i, chip).wait_recv()
        absorb(chip * 2 + 1 - core)

    def take(i):
        chip = gather.arrive(i)
        fwd_copy(i, chip).start()
        col_start(chip)
        return chip

    absorb_both(7, q)
    for i in (1, 2, 0, 4, 3):
        absorb_both(i, take(i))

    five = take(5)
    six = take(6)
    absorb_both(5, five)
    absorb_both(6, six)

    inv[...] = jnp.broadcast_to(
        lax.rsqrt(jnp.sum(ssq[...], axis=1, keepdims=True) * (1.0 / width) + EPS), inv.shape
    )
    for j in range(3):
        pre[j] = (acc[j] * inv[:, 0:1]).astype(BF16)

    mixer(
        pre, cot, taps, band, mix, gp, *halo,
    )

    seq_gather = Gather(
        lax.rem(s, 4), s // 4, lambda slot: gp_all.at[slot], lambda r, z: z * 4 + r,
        lambda r, z: {"seq": z * 4 + r}, gp_sem.at[0], gp_sem.at[1],
    )
    stat = jnp.zeros((tok, ch), F32)
    for j in range(3):
        value = gp[j].astype(F32)
        gp_all[s, j] = (value * inv[:, 0:1]).astype(BF16)
        stat += value * pre[j].astype(F32)
    seq_gather.start()

    eye = lax.broadcasted_iota(jnp.int32, (128, 128), 0) == lax.broadcasted_iota(jnp.int32, (128, 128), 1)

    stat = jnp.sum(stat, axis=1, keepdims=True)
    stats[0] = jnp.zeros((8, 128), F32)
    for h in range(tok // 128):
        piece = jnp.where(eye, stat[h * 128 : h * 128 + 128], 0.0)
        stats[0, h : h + 1, :] = jnp.sum(piece, axis=0, keepdims=True)
    stat_sib = remote(stats.at[0], stats.at[1], statp_sem, 0, {"tp": sib})
    stat_sib.start()

    def partial(rows_):
        value = None
        for j in range(3):
            term = lax.dot_general(
                gp[j], w[j, rows_, :], (((1,), (1,)), ((), ())), preferred_element_type=F32
            )
            value = term if value is None else value + term
        return value

    def sib_copy(i):
        return remote(sib_out.at[i], sib_in.at[i], sib_sem, i, {"tp": sib})

    def chunk_y(i):
        return lax.rem(y + 2 + i, 4)

    def pair_copy(i):
        return remote(pair_out.at[i], pair_in.at[i], pair_sem, i, {"tp": (chunk_y(i) * 2 + z_lo) * 2 + core})

    def across():
        return remote(pair_out.at[2], pair_in.at[2], pair_sem, 2, {"tp": (y * 2 + 1 - z_lo) * 2 + core})

    def finish(i):
        sib_copy(i).wait_recv()
        both = part[lax.rem(i, 2)] + sib_in[i].astype(F32)

        @pl.when(lax.rem(i, 4) == 2)
        def _():
            kept[i // 4] = both

        @pl.when(lax.rem(i, 4) != 2)
        def _():
            pair_out[i] = both.astype(BF16)
            pair_copy(i).start()

    def reduce(i):
        chip = chunk_y(i) * 2 + jnp.where(i < 4, 1 - z_lo, z_lo)
        sib_out[i] = partial(block_rows(chip * 2 + 1 - core)).astype(BF16)
        sib_copy(i).start()
        part[lax.rem(i, 2)] = partial(block_rows(chip * 2 + core))

        @pl.when(i > 0)
        def _():
            finish(i - 1)

    loop(0, chips, reduce)
    finish(chips - 1)
    for i in (1, 2, 0):
        seq_gather.arrive(i)
    for i in (0, 3, 1):
        pair_copy(i).wait_recv()
    pair_out[2] = (
        kept[0] + pair_in[0].astype(F32) + pair_in[1].astype(F32) + pair_in[3].astype(F32)
    ).astype(BF16)
    across().start()
    col_in(fetched(0)).wait_recv()
    for i in range(2):
        spread(i).start()


    stat_sib.wait_recv()
    stats[2] = stats[0] + stats[1]

    def stat_copy(k):
        return remote(stats.at[2], stats.at[2 + k], stat_sem, k, {"tp": tp_peer(k)})

    loop(1, chips, lambda k: stat_copy(k).start())

    def turn(chip):
        for half in range(2):
            cols_t[chip, half * own : half * own + own, :] = col[chip, half].T

    def product(source, begin=False):
        for j in range(3):
            term = jnp.dot(cols_t[source], gp_all[source, j], preferred_element_type=F32)
            total[j] = term if begin else total[j] + term

    for half in range(2):
        col[s, half] = ag[s * 2 + half, 0:tok, :]

    def pass_on(k):
        source = z_hi * 4 + lax.rem(x_at + k, 4)
        col_in(source).wait_recv()
        colf_copy(source).start()

    def turn_in(k):
        source = lax.rem(s + n_seq - k, n_seq)
        colf_in(source).wait_recv()
        turn(source)

    loop(1, 4, pass_on)
    turn(s)
    for i in (4, 3):
        seq_gather.arrive(i)
    for i in range(2):
        spread_in(i).wait_recv()
        spread(i + 2).start()
    for step in (0, -1, 1):
        colf_copy(fetched(step)).start()
    for i in (2, 3):
        spread_in(i).wait_recv()
    colf_copy(fetched(2)).start()
    loop(1, n_seq, turn_in)
    product(s, True)
    for i in (1, 2, 0, 4, 3):
        product(seq_gather.source(i))

    def collect(k):
        stat_copy(k).wait_recv()

    for i in (4, 5, 7):
        pair_copy(i).wait_recv()
    across().wait_recv()
    part[0] = (
        kept[1] + pair_in[4].astype(F32) + pair_in[5].astype(F32)
        + pair_in[7].astype(F32) + pair_in[2].astype(F32)
    )
    loop(1, chips, collect)
    stat_rows = sum(stats[2 + k] for k in range(chips)) * (1.0 / width)
    own_gain = ag[p, tok : tok + 16, :].astype(F32)[0:1]
    for h in range(tok // 128):
        r = slice(h * 128, h * 128 + 128)
        stat_col = jnp.sum(jnp.where(eye, stat_rows[h : h + 1, :], 0.0), axis=1, keepdims=True)
        rms = inv[r, 0:1]
        scaled = ag[p, r, :].astype(F32) * rms
        grad_in[r, :] = (rms * (own_gain * part[0, r, :] - scaled * stat_col)).astype(BF16)

    for i in (5, 6):
        product(seq_gather.arrive(i))
    for c in range(2 * own // 128):
        lane = (c * 128) % own
        g = ag[s * 2 + c * 128 // own, tok : tok + 16, lane : lane + 128].astype(F32)[0:1]
        g_col = jnp.sum(jnp.where(eye, g, 0.0), axis=1, keepdims=True)
        for j in range(3):
            grad_proj[j, c * 128 : c * 128 + 128, :] = (total[j, c * 128 : c * 128 + 128, :] * g_col).astype(BF16)

    def settle(k):
        @pl.when(k > 0)
        def _():
            stat_copy(k).wait_send()

        @pl.when(lax.rem(k, 4) != 2)
        def _():
            pair_copy(k).wait_send()

        sib_copy(k).wait_send()

        @pl.when(col_due(k))
        def _():
            col_send(k).wait_send()

        @pl.when(k != s)
        def _():
            colf_copy(k).wait_send()

    loop(0, chips, settle)
    across().wait_send()
    for i in range(4):
        spread(i).wait_send()
    for group in (gather, seq_gather):
        group.settle()
    for i in range(8):
        chip = q if i == 7 else gather.source(i)
        fwd_copy(i, chip).wait_send()
    stat_sib.wait_send()


def per_device(activations, norm_gain, in_proj, short_taps, medium_taps, cotangent):
    tok, own = activations.shape
    width, _, ch = in_proj.shape
    n_seq, n_tp = lax.axis_size("seq"), lax.axis_size("tp")
    chips = n_tp // 2
    vmem = pl.BlockSpec(memory_space=pltpu.VMEM)
    hbm = pl.BlockSpec(memory_space=pl.ANY)
    sems = lambda count: pltpu.SemaphoreType.DMA((2, count))
    mix, grad_in, grad_proj = pl.pallas_call(
        whole_kernel,
        out_shape=(
            jax.ShapeDtypeStruct((tok, ch), BF16),
            jax.ShapeDtypeStruct((tok, own), BF16),
            jax.ShapeDtypeStruct((3, 2 * own, ch), BF16),
        ),
        in_specs=[hbm] * 3 + [vmem] * 3,
        out_specs=(vmem,) * 3,
        scratch_shapes=[
            pltpu.VMEM((n_tp, tok + 16, own), BF16),
            pltpu.VMEM((3, width, ch), BF16),
            pltpu.VMEM((3, tok, ch), F32),
            pltpu.VMEM((tok, 128), F32),
            pltpu.VMEM((tok, 128), F32),
            pltpu.VMEM((3, tok, ch), BF16),
            pltpu.VMEM((3, tok, ch), BF16),
            pltpu.VMEM((n_seq, 2, tok, own), BF16),
            pltpu.VMEM((n_seq, 2 * own, tok), BF16),
            pltpu.VMEM((n_seq, 3, tok, ch), BF16),
            pltpu.VMEM((3, 2 * own, ch), F32),
            pltpu.VMEM((chips, tok, own), BF16),
            pltpu.VMEM((chips, tok, own), BF16),
            pltpu.VMEM((chips, tok, own), BF16),
            pltpu.VMEM((chips, tok, own), BF16),
            pltpu.VMEM((2, tok, own), F32),
            pltpu.VMEM((2, tok, own), F32),
            pltpu.VMEM((2 + chips, 8, 128), F32),
            pltpu.SemaphoreType.DMA((2,)),
            pltpu.SemaphoreType.DMA((n_tp,)),
            sems(7), sems(8), sems(n_seq), sems(4), sems(n_seq), sems(7), sems(chips), sems(chips), sems(chips), sems(1),
        ] + mixer_scratch(tok, ch),
        compiler_params=pltpu.CompilerParams(
            collective_id=0, has_side_effects=True, vmem_limit_bytes=60 * 2**20
        ),
    )(
        activations,
        jnp.broadcast_to(norm_gain[None], (16, own)),
        jnp.transpose(in_proj, (1, 0, 2)),
        cotangent,
        short_taps,
        medium_taps,
    )
    return mix, grad_in, jnp.transpose(grad_proj, (1, 0, 2))


def solution(mesh):
    return jax.shard_map(
        per_device,
        mesh=mesh,
        in_specs=(
            P("seq", "tp"), P("tp"), P(None, None, "tp"), P(None, None, "tp"), P("tp", None), P("seq", "tp"),
        ),
        out_specs=(P("seq", "tp"), P("seq", "tp"), P("seq", None, "tp")),
        check_vma=False,
    )
```

```python
import jax
import jax.numpy as jnp
from jax import lax
from jax.experimental import pallas as pl
from jax.experimental.pallas import tpu as pltpu
from jax.sharding import PartitionSpec as P

GROUP = 16
LM = 128
BLK = 128
EPS = 1e-06
F32 = jnp.float32
BF16 = jnp.bfloat16
MESH = pl.DeviceIdType.MESH


def build_bands(taps_ref, band_ref):
    groups = taps_ref.shape[0]

    def one(g, carry):
        row = jnp.broadcast_to(taps_ref[pl.ds(g, 1), :], (BLK, LM))
        wide = jnp.concatenate([row, jnp.zeros((BLK, BLK), F32)], 1)
        wide = pltpu.roll(wide, 0, 1, stride=1, stride_axis=0)
        band_ref[groups + g] = wide.astype(BF16)
        band_ref[g, :, 0:BLK] = wide[:, BLK:].T.astype(BF16)
        band_ref[g, :, BLK:] = wide[:, 0:BLK].T.astype(BF16)
        return carry

    lax.fori_loop(0, groups, one, 0)


def apply_band(band_ref, first, source_ref, row0):
    lane = lax.broadcasted_iota(jnp.int32, (BLK, 128), 1) // GROUP
    halves = source_ref.shape[1] // 128

    def one(g, totals):
        new = []
        for h in range(halves):
            part = jnp.dot(
                band_ref[first + h * 8 + g],
                source_ref[row0 : row0 + 2 * BLK, h * 128 : h * 128 + 128],
                preferred_element_type=F32,
            )
            new.append(jnp.where(lane == g, part, totals[h]))
        return tuple(new)

    totals = lax.fori_loop(0, 8, one, tuple(jnp.zeros((BLK, 128), F32) for _ in range(halves)))
    return jnp.concatenate(totals, 1)


def mixer(pre, cot, taps, band, mix, gp, ext, feat, gext, gfext, gft, ptail, ghead, gtail, send, recv):
    tok, ch = pre.shape[1], pre.shape[2]
    n = lax.axis_size("seq")
    me = lax.axis_index("seq")
    after, before = lax.rem(me + 1, n), lax.rem(me + n - 1, n)
    first, last = me == 0, me == n - 1
    groups = ch // GROUP

    def remote(src, dst, index, to):
        return pltpu.make_async_remote_copy(
            src_ref=src, dst_ref=dst, send_sem=send.at[index], recv_sem=recv.at[index],
            device_id={"seq": to}, device_id_type=MESH,
        )

    tail_copy = remote(pre.at[:, pl.ds(tok - 16, 16), :], ptail, 0, after)
    tail_copy.start()
    for j in range(3):
        ext[j, 8 : 8 + tok, :] = pre[j].astype(F32)

    def short(j, lo, hi):
        total = taps[0, j : j + 1, :] * ext[j, 8 + lo : 8 + hi, :]
        total += taps[1, j : j + 1, :] * ext[j, 7 + lo : 7 + hi, :]
        total += taps[2, j : j + 1, :] * ext[j, 6 + lo : 6 + hi, :]
        return total.astype(BF16)

    def gate(lo, hi):
        k, v = short(1, lo, hi), short(2, lo, hi)
        feat[1, lo:hi, :] = k
        feat[2, lo:hi, :] = v
        gext[BLK + lo : BLK + hi, :] = (k.astype(F32) * v.astype(F32)).astype(BF16)

    gate(tok - BLK, tok)
    gated_copy = remote(gext.at[pl.ds(tok, BLK), :], gext.at[pl.ds(0, BLK), :], 1, after)
    gated_copy.start()

    tail_copy.wait_recv()
    for j in range(3):
        ext[j, 0:8, :] = jnp.where(first, 0.0, ptail[j].astype(F32)[8:16])
    q = short(0, 0, tok)
    feat[0] = q
    grad_out = cot[...].astype(F32)
    gfext[0:tok, :] = (grad_out * q.astype(F32)).astype(BF16)
    filt_copy = remote(gfext.at[pl.ds(0, BLK), :], gtail, 2, before)
    filt_copy.start()
    gate(0, tok - BLK)

    def grad_kv(lo):
        gg = apply_band(band, groups, gfext, lo)
        gft[1, lo : lo + BLK, :] = (gg * feat[2, lo : lo + BLK, :].astype(F32)).astype(BF16).astype(F32)
        gft[2, lo : lo + BLK, :] = (gg * feat[1, lo : lo + BLK, :].astype(F32)).astype(BF16).astype(F32)

    def forward(lo):
        filt = apply_band(band, 0, gext, lo)
        mix[lo : lo + BLK, :] = (feat[0, lo : lo + BLK, :].astype(F32) * filt).astype(BF16)
        gft[0, lo : lo + BLK, :] = (cot[lo : lo + BLK, :].astype(F32) * filt).astype(BF16).astype(F32)

    grad_kv(0)
    gated_copy.wait_recv()

    @pl.when(first)
    def _():
        gext[0:BLK, :] = jnp.zeros((BLK, ch), BF16)

    forward(0)
    for j in range(3):
        ghead[0, j] = gft[j, 0:16, :].astype(BF16)
    head_copy = remote(ghead.at[0], ghead.at[1], 3, before)
    head_copy.start()
    forward(BLK)
    filt_copy.wait_recv()
    gfext[tok : tok + BLK, :] = jnp.where(last, 0.0, gtail[...].astype(F32)).astype(BF16)
    grad_kv(BLK)
    head_copy.wait_recv()
    for j in range(3):
        gft[j, tok : tok + 8, :] = jnp.where(last, 0.0, ghead[1, j].astype(F32)[0:8])
    for j in range(3):
        total = taps[0, j : j + 1, :] * gft[j, 0:tok, :]
        total += taps[1, j : j + 1, :] * gft[j, 1 : tok + 1, :]
        total += taps[2, j : j + 1, :] * gft[j, 2 : tok + 2, :]
        gp[j] = total.astype(BF16)
    for copy in (tail_copy, gated_copy, filt_copy, head_copy):
        copy.wait_send()


def mixer_scratch(tok, ch):
    return [
        pltpu.VMEM((2 * ch // GROUP, BLK, 2 * BLK), BF16),
        pltpu.VMEM((3, tok + 8, ch), F32),
        pltpu.VMEM((3, tok, ch), BF16),
        pltpu.VMEM((tok + BLK, ch), BF16),
        pltpu.VMEM((tok + BLK, ch), BF16),
        pltpu.VMEM((3, tok + 8, ch), F32),
        pltpu.VMEM((3, 16, ch), BF16),
        pltpu.VMEM((2, 3, 16, ch), BF16),
        pltpu.VMEM((BLK, ch), BF16),
        pltpu.SemaphoreType.DMA((4,)),
        pltpu.SemaphoreType.DMA((4,)),
    ]


class Gather:
    def __init__(self, ring, pair, block, slot, device, send, recv):
        self.ring, self.pair, self.block, self.slot, self.device = ring, pair, block, slot, device
        self.send, self.recv = send, recv

    def at(self, step, flip):
        ring = lax.rem(self.ring + step + 4, 4)
        return ring, (1 - self.pair if flip else self.pair)

    def source(self, i):
        where = ((0, 1), (-1, 0), (1, 0), (-1, 1), (1, 1), (2, 0), (2, 1))[i]
        return self.slot(*self.at(*where))

    def copy(self, i):
        what, to = (
            ((0, 0), (0, 1)), ((0, 0), (1, 0)), ((0, 0), (-1, 0)), ((0, 1), (1, 0)),
            ((0, 1), (-1, 0)), ((-1, 0), (1, 0)), ((1, 1), (-1, 0)),
        )[i]
        block = self.block(self.slot(*self.at(*what)))
        return pltpu.make_async_remote_copy(
            src_ref=block, dst_ref=block, send_sem=self.send.at[i], recv_sem=self.recv.at[i],
            device_id=self.device(*self.at(*to)), device_id_type=MESH,
        )

    def start(self):
        for i in (1, 2, 0):
            self.copy(i).start()

    def arrive(self, i):
        block = self.block(self.source(i))
        pltpu.make_async_remote_copy(
            src_ref=block, dst_ref=block, send_sem=self.send.at[i], recv_sem=self.recv.at[i],
            device_id=self.device(*self.at(0, 1)), device_id_type=MESH,
        ).wait_recv()
        for following in {0: (3, 4), 1: (5,), 4: (6,)}.get(i, ()):
            self.copy(following).start()
        return self.source(i)

    def settle(self):
        for i in range(7):
            self.copy(i).wait_send()


def whole_kernel(
    act, gain, weight, cot, taps, medium, mix, grad_in, grad_proj,
    ag, w, acc, ssq, inv, pre, gp, col, cols_t, gp_all, total, sib_out, sib_in, pair_out, pair_in, part, kept, stats,
    load_sem, w_sem, ag_sem, fwd_sem, col_sem, spread_sem, colf_sem, gp_sem, sib_sem, pair_sem, stat_sem, statp_sem,
    band, *halo,
):
    n_seq, n_tp = lax.axis_size("seq"), lax.axis_size("tp")
    tok, own = act.shape
    ch = pre.shape[2]
    chips = n_tp // 2
    s, p = lax.axis_index("seq"), lax.axis_index("tp")
    q, core = p // 2, lax.rem(p, 2)
    sib = p + 1 - 2 * core
    width = n_tp * own

    def remote(src, dst, sems, index, to):
        return pltpu.make_async_remote_copy(
            src_ref=src, dst_ref=dst, send_sem=sems.at[0, index], recv_sem=sems.at[1, index],
            device_id=to, device_id_type=MESH,
        )

    def tp_peer(k):
        return lax.rem(q + k, chips) * 2 + core

    def loop(lo, hi, body):
        def step(i, carry):
            body(i)
            return carry

        lax.fori_loop(lo, hi, step, 0)

    def block_rows(index):
        return pl.ds(pl.multiple_of(index * own, own), own)

    loads = (
        pltpu.make_async_copy(act, ag.at[p, pl.ds(0, tok), :], load_sem.at[0]),
        pltpu.make_async_copy(gain, ag.at[p, pl.ds(tok, 16), :], load_sem.at[1]),
    )
    for copy in loads:
        copy.start()

    def w_copy(index):
        return pltpu.make_async_copy(
            weight.at[:, block_rows(index), :], w.at[:, block_rows(index), :], w_sem.at[index]
        )

    loop(0, n_tp, lambda i: w_copy(lax.rem(p + i, n_tp)).start())

    barrier = pltpu.get_barrier_semaphore()

    def greet(k):
        pl.semaphore_signal(barrier, inc=1, device_id={"seq": s, "tp": tp_peer(k)}, device_id_type=MESH)
        to = lax.rem(s + k, n_seq)
        pl.semaphore_signal(barrier, inc=1, device_id={"seq": to, "tp": p}, device_id_type=MESH)

    loop(1, 8, greet)
    pl.semaphore_signal(barrier, inc=1, device_id={"seq": s, "tp": sib}, device_id_type=MESH)

    for copy in loads:
        copy.wait()
    pl.semaphore_wait(barrier, 15)

    y, z_lo = q // 2, lax.rem(q, 2)
    gather = Gather(
        y, z_lo, lambda chip: ag.at[chip * 2 + core], lambda r, z: r * 2 + z,
        lambda r, z: {"tp": (r * 2 + z) * 2 + core}, ag_sem.at[0], ag_sem.at[1],
    )
    gather.start()

    z_hi, x_at = s // 4, lax.rem(s, 4)
    def col_send(to):
        return pltpu.make_async_remote_copy(
            src_ref=ag.at[to * 2 + core, pl.ds(0, tok), :], dst_ref=col.at[s, core],
            send_sem=col_sem.at[0, to], recv_sem=col_sem.at[1, s],
            device_id={"seq": to}, device_id_type=MESH,
        )

    def col_in(source):
        return pltpu.make_async_remote_copy(
            src_ref=col.at[source, core], dst_ref=col.at[source, core],
            send_sem=col_sem.at[0, source], recv_sem=col_sem.at[1, source],
            device_id={"seq": source}, device_id_type=MESH,
        )

    def col_due(chip):
        near = chip // 4 == z_hi
        return (near & (lax.rem(chip, 4) != x_at)) | (~near & (lax.rem(chip + y, 4) == x_at))

    def col_start(chip):
        @pl.when(col_due(chip))
        def _():
            col_send(chip).start()

    def fetched(step):
        return (1 - z_hi) * 4 + lax.rem(x_at + y + step + 4, 4)

    def spread(i):
        step, part_rows, to = (
            (0, pl.ds(0, tok), 1), (0, pl.ds(0, tok), 3), (-1, pl.ds(0, tok // 2), 1), (1, pl.ds(tok // 2, tok // 2), 3),
        )[i]
        block = col.at[fetched(step), core, part_rows, :]
        return remote(block, block, spread_sem, i, {"tp": (lax.rem(y + to, 4) * 2 + z_lo) * 2 + core})

    def spread_in(i):
        step, part_rows = (
            (-1, pl.ds(0, tok)), (1, pl.ds(0, tok)), (2, pl.ds(0, tok // 2)), (2, pl.ds(tok // 2, tok // 2)),
        )[i]
        block = col.at[fetched(step), core, part_rows, :]
        return remote(block, block, spread_sem, i, {"tp": sib})

    def fwd_copy(i, chip):
        slot = chip * 2 + core
        return remote(ag.at[slot], ag.at[slot], fwd_sem, i, {"tp": sib})

    def fwd_in(i, chip):
        slot = chip * 2 + 1 - core
        return remote(ag.at[slot], ag.at[slot], fwd_sem, i, {"tp": sib})

    def colf_copy(source):
        return remote(col.at[source, core], col.at[source, core], colf_sem, source, {"tp": sib})

    def colf_in(source):
        return remote(col.at[source, 1 - core], col.at[source, 1 - core], colf_sem, source, {"tp": sib})

    col_start(q)
    fwd_copy(7, q).start()
    build_bands(medium, band)
    acc[...] = jnp.zeros_like(acc)
    ssq[...] = jnp.zeros_like(ssq)

    def absorb(slot):
        w_copy(slot).wait()
        x = ag[slot, 0:tok, :].astype(F32)
        g = ag[slot, tok : tok + 16, :].astype(F32)[0:1]
        square = x * x
        ssq[...] += sum(square[:, i * 128 : i * 128 + 128] for i in range(own // 128))
        scaled = (x * g).astype(BF16)
        for j in range(3):
            acc[j] += jnp.dot(scaled, w[j, block_rows(slot), :], preferred_element_type=F32)

    def absorb_both(i, chip):
        absorb(chip * 2 + core)
        fwd_in(i, chip).wait_recv()
        absorb(chip * 2 + 1 - core)

    def take(i):
        chip = gather.arrive(i)
        fwd_copy(i, chip).start()
        col_start(chip)
        return chip

    absorb_both(7, q)
    for i in (1, 2, 0, 4, 3):
        absorb_both(i, take(i))

    five = take(5)
    six = take(6)
    absorb_both(5, five)
    absorb_both(6, six)

    inv[...] = jnp.broadcast_to(
        lax.rsqrt(jnp.sum(ssq[...], axis=1, keepdims=True) * (1.0 / width) + EPS), inv.shape
    )
    for j in range(3):
        pre[j] = (acc[j] * inv[:, 0:1]).astype(BF16)

    mixer(
        pre, cot, taps, band, mix, gp, *halo,
    )

    seq_gather = Gather(
        lax.rem(s, 4), s // 4, lambda slot: gp_all.at[slot], lambda r, z: z * 4 + r,
        lambda r, z: {"seq": z * 4 + r}, gp_sem.at[0], gp_sem.at[1],
    )
    stat = jnp.zeros((tok, ch), F32)
    for j in range(3):
        value = gp[j].astype(F32)
        gp_all[s, j] = (value * inv[:, 0:1]).astype(BF16)
        stat += value * pre[j].astype(F32)
    seq_gather.start()
    col_in(fetched(0)).wait_recv()
    for i in range(2):
        spread(i).start()


    eye = lax.broadcasted_iota(jnp.int32, (128, 128), 0) == lax.broadcasted_iota(jnp.int32, (128, 128), 1)

    stat = jnp.sum(stat, axis=1, keepdims=True)
    stats[0] = jnp.zeros((8, 128), F32)
    for h in range(tok // 128):
        piece = jnp.where(eye, stat[h * 128 : h * 128 + 128], 0.0)
        stats[0, h : h + 1, :] = jnp.sum(piece, axis=0, keepdims=True)
    stat_sib = remote(stats.at[0], stats.at[1], statp_sem, 0, {"tp": sib})
    stat_sib.start()

    def partial(rows_):
        value = None
        for j in range(3):
            term = lax.dot_general(
                gp[j], w[j, rows_, :], (((1,), (1,)), ((), ())), preferred_element_type=F32
            )
            value = term if value is None else value + term
        return value

    def sib_copy(i):
        return remote(sib_out.at[i], sib_in.at[i], sib_sem, i, {"tp": sib})

    def chunk_y(i):
        return lax.rem(y + 2 + i, 4)

    def pair_copy(i):
        return remote(pair_out.at[i], pair_in.at[i], pair_sem, i, {"tp": (chunk_y(i) * 2 + z_lo) * 2 + core})

    def across():
        return remote(pair_out.at[2], pair_in.at[2], pair_sem, 2, {"tp": (y * 2 + 1 - z_lo) * 2 + core})

    def finish(i):
        sib_copy(i).wait_recv()
        both = part[lax.rem(i, 2)] + sib_in[i].astype(F32)

        @pl.when(lax.rem(i, 4) == 2)
        def _():
            kept[i // 4] = both

        @pl.when(lax.rem(i, 4) != 2)
        def _():
            pair_out[i] = both.astype(BF16)
            pair_copy(i).start()

    def reduce(i):
        chip = chunk_y(i) * 2 + jnp.where(i < 4, 1 - z_lo, z_lo)
        sib_out[i] = partial(block_rows(chip * 2 + 1 - core)).astype(BF16)
        sib_copy(i).start()
        part[lax.rem(i, 2)] = partial(block_rows(chip * 2 + core))

        @pl.when(i > 0)
        def _():
            finish(i - 1)

    loop(0, chips, reduce)
    finish(chips - 1)
    for i in range(2):
        spread_in(i).wait_recv()
        spread(i + 2).start()
    for i in (1, 2, 0):
        seq_gather.arrive(i)
    for i in (0, 3, 1):
        pair_copy(i).wait_recv()
    pair_out[2] = (
        kept[0] + pair_in[0].astype(F32) + pair_in[1].astype(F32) + pair_in[3].astype(F32)
    ).astype(BF16)
    across().start()

    stat_sib.wait_recv()
    stats[2] = stats[0] + stats[1]

    def stat_copy(k):
        return remote(stats.at[2], stats.at[2 + k], stat_sem, k, {"tp": tp_peer(k)})

    loop(1, chips, lambda k: stat_copy(k).start())

    def turn(chip):
        for half in range(2):
            cols_t[chip, half * own : half * own + own, :] = col[chip, half].T

    def product(source, begin=False):
        for j in range(3):
            term = jnp.dot(cols_t[source], gp_all[source, j], preferred_element_type=F32)
            total[j] = term if begin else total[j] + term

    for half in range(2):
        col[s, half] = ag[s * 2 + half, 0:tok, :]

    def pass_on(k):
        source = z_hi * 4 + lax.rem(x_at + k, 4)
        col_in(source).wait_recv()
        colf_copy(source).start()

    def turn_in(k):
        source = lax.rem(s + n_seq - k, n_seq)
        colf_in(source).wait_recv()
        turn(source)

    loop(1, 4, pass_on)
    turn(s)
    for i in (4, 3):
        seq_gather.arrive(i)
    for step in (0, -1, 1):
        colf_copy(fetched(step)).start()
    for i in (2, 3):
        spread_in(i).wait_recv()
    colf_copy(fetched(2)).start()
    loop(1, n_seq, turn_in)
    product(s, True)
    for i in (1, 2, 0, 4, 3):
        product(seq_gather.source(i))

    def collect(k):
        stat_copy(k).wait_recv()

    for i in (4, 5, 7):
        pair_copy(i).wait_recv()
    across().wait_recv()
    part[0] = (
        kept[1] + pair_in[4].astype(F32) + pair_in[5].astype(F32)
        + pair_in[7].astype(F32) + pair_in[2].astype(F32)
    )
    loop(1, chips, collect)
    stat_rows = sum(stats[2 + k] for k in range(chips)) * (1.0 / width)
    own_gain = ag[p, tok : tok + 16, :].astype(F32)[0:1]
    for h in range(tok // 128):
        r = slice(h * 128, h * 128 + 128)
        stat_col = jnp.sum(jnp.where(eye, stat_rows[h : h + 1, :], 0.0), axis=1, keepdims=True)
        rms = inv[r, 0:1]
        scaled = ag[p, r, :].astype(F32) * rms
        grad_in[r, :] = (rms * (own_gain * part[0, r, :] - scaled * stat_col)).astype(BF16)

    for i in (5, 6):
        product(seq_gather.arrive(i))
    for c in range(2 * own // 128):
        lane = (c * 128) % own
        g = ag[s * 2 + c * 128 // own, tok : tok + 16, lane : lane + 128].astype(F32)[0:1]
        g_col = jnp.sum(jnp.where(eye, g, 0.0), axis=1, keepdims=True)
        for j in range(3):
            grad_proj[j, c * 128 : c * 128 + 128, :] = (total[j, c * 128 : c * 128 + 128, :] * g_col).astype(BF16)

    def settle(k):
        @pl.when(k > 0)
        def _():
            stat_copy(k).wait_send()

        @pl.when(lax.rem(k, 4) != 2)
        def _():
            pair_copy(k).wait_send()

        sib_copy(k).wait_send()

        @pl.when(col_due(k))
        def _():
            col_send(k).wait_send()

        @pl.when(k != s)
        def _():
            colf_copy(k).wait_send()

    loop(0, chips, settle)
    across().wait_send()
    for i in range(4):
        spread(i).wait_send()
    for group in (gather, seq_gather):
        group.settle()
    for i in range(8):
        chip = q if i == 7 else gather.source(i)
        fwd_copy(i, chip).wait_send()
    stat_sib.wait_send()


def hand_over(*refs):
    for source, target in zip(refs[:3], refs[3:]):
        target[...] = source[...]


def per_device(activations, norm_gain, in_proj, short_taps, medium_taps, cotangent):
    tok, own = activations.shape
    width, _, ch = in_proj.shape
    n_seq, n_tp = lax.axis_size("seq"), lax.axis_size("tp")
    chips = n_tp // 2
    vmem = pl.BlockSpec(memory_space=pltpu.VMEM)
    hbm = pl.BlockSpec(memory_space=pl.ANY)
    sems = lambda count: pltpu.SemaphoreType.DMA((2, count))
    mix, grad_in, grad_proj = pl.pallas_call(
        whole_kernel,
        out_shape=(
            jax.ShapeDtypeStruct((tok, ch), BF16),
            jax.ShapeDtypeStruct((tok, own), BF16),
            jax.ShapeDtypeStruct((3, 2 * own, ch), BF16),
        ),
        in_specs=[hbm] * 3 + [vmem] * 3,
        out_specs=(vmem,) * 3,
        scratch_shapes=[
            pltpu.VMEM((n_tp, tok + 16, own), BF16),
            pltpu.VMEM((3, width, ch), BF16),
            pltpu.VMEM((3, tok, ch), F32),
            pltpu.VMEM((tok, 128), F32),
            pltpu.VMEM((tok, 128), F32),
            pltpu.VMEM((3, tok, ch), BF16),
            pltpu.VMEM((3, tok, ch), BF16),
            pltpu.VMEM((n_seq, 2, tok, own), BF16),
            pltpu.VMEM((n_seq, 2 * own, tok), BF16),
            pltpu.VMEM((n_seq, 3, tok, ch), BF16),
            pltpu.VMEM((3, 2 * own, ch), F32),
            pltpu.VMEM((chips, tok, own), BF16),
            pltpu.VMEM((chips, tok, own), BF16),
            pltpu.VMEM((chips, tok, own), BF16),
            pltpu.VMEM((chips, tok, own), BF16),
            pltpu.VMEM((2, tok, own), F32),
            pltpu.VMEM((2, tok, own), F32),
            pltpu.VMEM((2 + chips, 8, 128), F32),
            pltpu.SemaphoreType.DMA((2,)),
            pltpu.SemaphoreType.DMA((n_tp,)),
            sems(7), sems(8), sems(n_seq), sems(4), sems(n_seq), sems(7), sems(chips), sems(chips), sems(chips), sems(1),
        ] + mixer_scratch(tok, ch),
        compiler_params=pltpu.CompilerParams(
            collective_id=0, has_side_effects=True, vmem_limit_bytes=60 * 2**20
        ),
    )(
        activations,
        jnp.broadcast_to(norm_gain[None], (16, own)),
        jnp.transpose(in_proj, (1, 0, 2)),
        cotangent,
        short_taps,
        medium_taps,
    )
    results = (mix, grad_in, grad_proj)
    mix, grad_in, grad_proj = pl.pallas_call(
        hand_over,
        out_shape=tuple(jax.ShapeDtypeStruct(a.shape, a.dtype) for a in results),
        in_specs=[vmem] * 3,
        out_specs=(vmem,) * 3,
    )(*results)
    return mix, grad_in, jnp.transpose(grad_proj, (1, 0, 2))


def solution(mesh):
    return jax.shard_map(
        per_device,
        mesh=mesh,
        in_specs=(
            P("seq", "tp"), P("tp"), P(None, None, "tp"), P(None, None, "tp"), P("tp", None), P("seq", "tp"),
        ),
        out_specs=(P("seq", "tp"), P("seq", "tp"), P("seq", None, "tp")),
        check_vma=False,
    )
```

```python
import jax
import jax.numpy as jnp
from jax import lax
from jax.experimental import pallas as pl
from jax.experimental.pallas import tpu as pltpu
from jax.sharding import PartitionSpec as P

GROUP = 16
LM = 128
BLK = 128
EPS = 1e-06
F32 = jnp.float32
BF16 = jnp.bfloat16
MESH = pl.DeviceIdType.MESH


def build_bands(taps_ref, band_ref):
    groups = taps_ref.shape[0]

    def one(g, carry):
        row = jnp.broadcast_to(taps_ref[pl.ds(g, 1), :], (BLK, LM))
        wide = jnp.concatenate([row, jnp.zeros((BLK, BLK), F32)], 1)
        wide = pltpu.roll(wide, 0, 1, stride=1, stride_axis=0)
        band_ref[groups + g] = wide.astype(BF16)
        band_ref[g, :, 0:BLK] = wide[:, BLK:].T.astype(BF16)
        band_ref[g, :, BLK:] = wide[:, 0:BLK].T.astype(BF16)
        return carry

    lax.fori_loop(0, groups, one, 0)


def apply_band(band_ref, first, source_ref, row0):
    lane = lax.broadcasted_iota(jnp.int32, (BLK, 128), 1) // GROUP
    halves = source_ref.shape[1] // 128

    def one(g, totals):
        new = []
        for h in range(halves):
            part = jnp.dot(
                band_ref[first + h * 8 + g],
                source_ref[row0 : row0 + 2 * BLK, h * 128 : h * 128 + 128],
                preferred_element_type=F32,
            )
            new.append(jnp.where(lane == g, part, totals[h]))
        return tuple(new)

    totals = lax.fori_loop(0, 8, one, tuple(jnp.zeros((BLK, 128), F32) for _ in range(halves)))
    return jnp.concatenate(totals, 1)


def mixer(pre, cot, taps, band, mix, gp, ext, feat, gext, gfext, gft, ptail, ghead, gtail, send, recv):
    tok, ch = pre.shape[1], pre.shape[2]
    n = lax.axis_size("seq")
    me = lax.axis_index("seq")
    after, before = lax.rem(me + 1, n), lax.rem(me + n - 1, n)
    first, last = me == 0, me == n - 1
    groups = ch // GROUP

    def remote(src, dst, index, to):
        return pltpu.make_async_remote_copy(
            src_ref=src, dst_ref=dst, send_sem=send.at[index], recv_sem=recv.at[index],
            device_id={"seq": to}, device_id_type=MESH,
        )

    tail_copy = remote(pre.at[:, pl.ds(tok - 16, 16), :], ptail, 0, after)
    tail_copy.start()
    for j in range(3):
        ext[j, 8 : 8 + tok, :] = pre[j].astype(F32)

    def short(j, lo, hi):
        total = taps[0, j : j + 1, :] * ext[j, 8 + lo : 8 + hi, :]
        total += taps[1, j : j + 1, :] * ext[j, 7 + lo : 7 + hi, :]
        total += taps[2, j : j + 1, :] * ext[j, 6 + lo : 6 + hi, :]
        return total.astype(BF16)

    def gate(lo, hi):
        k, v = short(1, lo, hi), short(2, lo, hi)
        feat[1, lo:hi, :] = k
        feat[2, lo:hi, :] = v
        gext[BLK + lo : BLK + hi, :] = (k.astype(F32) * v.astype(F32)).astype(BF16)

    gate(tok - BLK, tok)
    gated_copy = remote(gext.at[pl.ds(tok, BLK), :], gext.at[pl.ds(0, BLK), :], 1, after)
    gated_copy.start()

    tail_copy.wait_recv()
    for j in range(3):
        ext[j, 0:8, :] = jnp.where(first, 0.0, ptail[j].astype(F32)[8:16])
    q = short(0, 0, tok)
    feat[0] = q
    grad_out = cot[...].astype(F32)
    gfext[0:tok, :] = (grad_out * q.astype(F32)).astype(BF16)
    filt_copy = remote(gfext.at[pl.ds(0, BLK), :], gtail, 2, before)
    filt_copy.start()
    gate(0, tok - BLK)

    def grad_kv(lo):
        gg = apply_band(band, groups, gfext, lo)
        gft[1, lo : lo + BLK, :] = (gg * feat[2, lo : lo + BLK, :].astype(F32)).astype(BF16).astype(F32)
        gft[2, lo : lo + BLK, :] = (gg * feat[1, lo : lo + BLK, :].astype(F32)).astype(BF16).astype(F32)

    def forward(lo):
        filt = apply_band(band, 0, gext, lo)
        mix[lo : lo + BLK, :] = (feat[0, lo : lo + BLK, :].astype(F32) * filt).astype(BF16)
        gft[0, lo : lo + BLK, :] = (cot[lo : lo + BLK, :].astype(F32) * filt).astype(BF16).astype(F32)

    grad_kv(0)
    gated_copy.wait_recv()

    @pl.when(first)
    def _():
        gext[0:BLK, :] = jnp.zeros((BLK, ch), BF16)

    forward(0)
    for j in range(3):
        ghead[0, j] = gft[j, 0:16, :].astype(BF16)
    head_copy = remote(ghead.at[0], ghead.at[1], 3, before)
    head_copy.start()
    forward(BLK)
    filt_copy.wait_recv()
    gfext[tok : tok + BLK, :] = jnp.where(last, 0.0, gtail[...].astype(F32)).astype(BF16)
    grad_kv(BLK)
    head_copy.wait_recv()
    for j in range(3):
        gft[j, tok : tok + 8, :] = jnp.where(last, 0.0, ghead[1, j].astype(F32)[0:8])
    for j in range(3):
        total = taps[0, j : j + 1, :] * gft[j, 0:tok, :]
        total += taps[1, j : j + 1, :] * gft[j, 1 : tok + 1, :]
        total += taps[2, j : j + 1, :] * gft[j, 2 : tok + 2, :]
        gp[j] = total.astype(BF16)
    for copy in (tail_copy, gated_copy, filt_copy, head_copy):
        copy.wait_send()


def mixer_scratch(tok, ch):
    return [
        pltpu.VMEM((2 * ch // GROUP, BLK, 2 * BLK), BF16),
        pltpu.VMEM((3, tok + 8, ch), F32),
        pltpu.VMEM((3, tok, ch), BF16),
        pltpu.VMEM((tok + BLK, ch), BF16),
        pltpu.VMEM((tok + BLK, ch), BF16),
        pltpu.VMEM((3, tok + 8, ch), F32),
        pltpu.VMEM((3, 16, ch), BF16),
        pltpu.VMEM((2, 3, 16, ch), BF16),
        pltpu.VMEM((BLK, ch), BF16),
        pltpu.SemaphoreType.DMA((4,)),
        pltpu.SemaphoreType.DMA((4,)),
    ]


class Gather:
    def __init__(self, ring, pair, block, slot, device, send, recv):
        self.ring, self.pair, self.block, self.slot, self.device = ring, pair, block, slot, device
        self.send, self.recv = send, recv

    def at(self, step, flip):
        ring = lax.rem(self.ring + step + 4, 4)
        return ring, (1 - self.pair if flip else self.pair)

    def source(self, i):
        where = ((0, 1), (-1, 0), (1, 0), (-1, 1), (1, 1), (2, 0), (2, 1))[i]
        return self.slot(*self.at(*where))

    def copy(self, i):
        what, to = (
            ((0, 0), (0, 1)), ((0, 0), (1, 0)), ((0, 0), (-1, 0)), ((0, 1), (1, 0)),
            ((0, 1), (-1, 0)), ((-1, 0), (1, 0)), ((1, 1), (-1, 0)),
        )[i]
        block = self.block(self.slot(*self.at(*what)))
        return pltpu.make_async_remote_copy(
            src_ref=block, dst_ref=block, send_sem=self.send.at[i], recv_sem=self.recv.at[i],
            device_id=self.device(*self.at(*to)), device_id_type=MESH,
        )

    def start(self):
        for i in range(3):
            self.copy(i).start()

    def arrive(self, i):
        block = self.block(self.source(i))
        pltpu.make_async_remote_copy(
            src_ref=block, dst_ref=block, send_sem=self.send.at[i], recv_sem=self.recv.at[i],
            device_id=self.device(*self.at(0, 1)), device_id_type=MESH,
        ).wait_recv()
        for following in {0: (3, 4), 1: (5,), 4: (6,)}.get(i, ()):
            self.copy(following).start()
        return self.source(i)

    def settle(self):
        for i in range(7):
            self.copy(i).wait_send()


def whole_kernel(
    act, gain, weight, cot, taps, medium, mix, grad_in, grad_proj,
    ag, w, acc, ssq, inv, pre, gp, col, cols_t, gp_all, total, sib_out, sib_in, pair_out, pair_in, part, kept, stats,
    load_sem, w_sem, ag_sem, fwd_sem, col_sem, spread_sem, colf_sem, gp_sem, sib_sem, pair_sem, stat_sem, statp_sem,
    band, *halo,
):
    n_seq, n_tp = lax.axis_size("seq"), lax.axis_size("tp")
    tok, own = act.shape
    ch = pre.shape[2]
    chips = n_tp // 2
    s, p = lax.axis_index("seq"), lax.axis_index("tp")
    q, core = p // 2, lax.rem(p, 2)
    sib = p + 1 - 2 * core
    width = n_tp * own

    def remote(src, dst, sems, index, to):
        return pltpu.make_async_remote_copy(
            src_ref=src, dst_ref=dst, send_sem=sems.at[0, index], recv_sem=sems.at[1, index],
            device_id=to, device_id_type=MESH,
        )

    def tp_peer(k):
        return lax.rem(q + k, chips) * 2 + core

    def loop(lo, hi, body):
        def step(i, carry):
            body(i)
            return carry

        lax.fori_loop(lo, hi, step, 0)

    def block_rows(index):
        return pl.ds(pl.multiple_of(index * own, own), own)

    loads = (
        pltpu.make_async_copy(act, ag.at[p, pl.ds(0, tok), :], load_sem.at[0]),
        pltpu.make_async_copy(gain, ag.at[p, pl.ds(tok, 16), :], load_sem.at[1]),
    )
    for copy in loads:
        copy.start()

    def w_copy(index):
        return pltpu.make_async_copy(
            weight.at[:, block_rows(index), :], w.at[:, block_rows(index), :], w_sem.at[index]
        )

    loop(0, n_tp, lambda i: w_copy(lax.rem(p + i, n_tp)).start())

    barrier = pltpu.get_barrier_semaphore()

    def greet(k):
        pl.semaphore_signal(barrier, inc=1, device_id={"seq": s, "tp": tp_peer(k)}, device_id_type=MESH)
        to = lax.rem(s + k, n_seq)
        pl.semaphore_signal(barrier, inc=1, device_id={"seq": to, "tp": p}, device_id_type=MESH)

    loop(1, 8, greet)
    pl.semaphore_signal(barrier, inc=1, device_id={"seq": s, "tp": sib}, device_id_type=MESH)

    for copy in loads:
        copy.wait()
    pl.semaphore_wait(barrier, 15)

    y, z_lo = q // 2, lax.rem(q, 2)
    gather = Gather(
        y, z_lo, lambda chip: ag.at[chip * 2 + core], lambda r, z: r * 2 + z,
        lambda r, z: {"tp": (r * 2 + z) * 2 + core}, ag_sem.at[0], ag_sem.at[1],
    )
    gather.start()

    z_hi, x_at = s // 4, lax.rem(s, 4)
    def col_send(to):
        return pltpu.make_async_remote_copy(
            src_ref=ag.at[to * 2 + core, pl.ds(0, tok), :], dst_ref=col.at[s, core],
            send_sem=col_sem.at[0, to], recv_sem=col_sem.at[1, s],
            device_id={"seq": to}, device_id_type=MESH,
        )

    def col_in(source):
        return pltpu.make_async_remote_copy(
            src_ref=col.at[source, core], dst_ref=col.at[source, core],
            send_sem=col_sem.at[0, source], recv_sem=col_sem.at[1, source],
            device_id={"seq": source}, device_id_type=MESH,
        )

    def col_due(chip):
        near = chip // 4 == z_hi
        return (near & (lax.rem(chip, 4) != x_at)) | (~near & (lax.rem(chip + y, 4) == x_at))

    def col_start(chip):
        @pl.when(col_due(chip))
        def _():
            col_send(chip).start()

    def fetched(step):
        return (1 - z_hi) * 4 + lax.rem(x_at + y + step + 4, 4)

    def spread(i):
        step, part_rows, to = (
            (0, pl.ds(0, tok), 1), (0, pl.ds(0, tok), 3), (-1, pl.ds(0, tok // 2), 1), (1, pl.ds(tok // 2, tok // 2), 3),
        )[i]
        block = col.at[fetched(step), core, part_rows, :]
        return remote(block, block, spread_sem, i, {"tp": (lax.rem(y + to, 4) * 2 + z_lo) * 2 + core})

    def spread_in(i):
        step, part_rows = (
            (-1, pl.ds(0, tok)), (1, pl.ds(0, tok)), (2, pl.ds(0, tok // 2)), (2, pl.ds(tok // 2, tok // 2)),
        )[i]
        block = col.at[fetched(step), core, part_rows, :]
        return remote(block, block, spread_sem, i, {"tp": sib})

    def fwd_copy(i, chip):
        slot = chip * 2 + core
        return remote(ag.at[slot], ag.at[slot], fwd_sem, i, {"tp": sib})

    def fwd_in(i, chip):
        slot = chip * 2 + 1 - core
        return remote(ag.at[slot], ag.at[slot], fwd_sem, i, {"tp": sib})

    def colf_copy(source):
        return remote(col.at[source, core], col.at[source, core], colf_sem, source, {"tp": sib})

    def colf_in(source):
        return remote(col.at[source, 1 - core], col.at[source, 1 - core], colf_sem, source, {"tp": sib})

    col_start(q)
    fwd_copy(7, q).start()
    build_bands(medium, band)
    acc[...] = jnp.zeros_like(acc)
    ssq[...] = jnp.zeros_like(ssq)

    def absorb(slot):
        w_copy(slot).wait()
        x = ag[slot, 0:tok, :].astype(F32)
        g = ag[slot, tok : tok + 16, :].astype(F32)[0:1]
        square = x * x
        ssq[...] += sum(square[:, i * 128 : i * 128 + 128] for i in range(own // 128))
        scaled = (x * g).astype(BF16)
        for j in range(3):
            acc[j] += jnp.dot(scaled, w[j, block_rows(slot), :], preferred_element_type=F32)

    def absorb_both(i, chip):
        absorb(chip * 2 + core)
        fwd_in(i, chip).wait_recv()
        absorb(chip * 2 + 1 - core)

    def take(i):
        chip = gather.arrive(i)
        fwd_copy(i, chip).start()
        col_start(chip)
        return chip

    absorb_both(7, q)
    for batch in ((0, 1, 2), (4, 3)):
        chips_in = [take(i) for i in batch]
        for i, chip in zip(batch, chips_in):
            absorb_both(i, chip)

    five = take(5)
    six = take(6)
    absorb_both(5, five)
    absorb_both(6, six)

    inv[...] = jnp.broadcast_to(
        lax.rsqrt(jnp.sum(ssq[...], axis=1, keepdims=True) * (1.0 / width) + EPS), inv.shape
    )
    for j in range(3):
        pre[j] = (acc[j] * inv[:, 0:1]).astype(BF16)

    mixer(
        pre, cot, taps, band, mix, gp, *halo,
    )

    seq_gather = Gather(
        lax.rem(s, 4), s // 4, lambda slot: gp_all.at[slot], lambda r, z: z * 4 + r,
        lambda r, z: {"seq": z * 4 + r}, gp_sem.at[0], gp_sem.at[1],
    )
    stat = jnp.zeros((tok, ch), F32)
    for j in range(3):
        value = gp[j].astype(F32)
        gp_all[s, j] = (value * inv[:, 0:1]).astype(BF16)
        stat += value * pre[j].astype(F32)
    seq_gather.start()
    col_in(fetched(0)).wait_recv()
    for i in range(2):
        spread(i).start()


    eye = lax.broadcasted_iota(jnp.int32, (128, 128), 0) == lax.broadcasted_iota(jnp.int32, (128, 128), 1)

    stat = jnp.sum(stat, axis=1, keepdims=True)
    stats[0] = jnp.zeros((8, 128), F32)
    for h in range(tok // 128):
        piece = jnp.where(eye, stat[h * 128 : h * 128 + 128], 0.0)
        stats[0, h : h + 1, :] = jnp.sum(piece, axis=0, keepdims=True)
    stat_sib = remote(stats.at[0], stats.at[1], statp_sem, 0, {"tp": sib})
    stat_sib.start()

    def partial(rows_):
        value = None
        for j in range(3):
            term = lax.dot_general(
                gp[j], w[j, rows_, :], (((1,), (1,)), ((), ())), preferred_element_type=F32
            )
            value = term if value is None else value + term
        return value

    def sib_copy(i):
        return remote(sib_out.at[i], sib_in.at[i], sib_sem, i, {"tp": sib})

    def chunk_y(i):
        return lax.rem(y + 2 + i, 4)

    def pair_copy(i):
        return remote(pair_out.at[i], pair_in.at[i], pair_sem, i, {"tp": (chunk_y(i) * 2 + z_lo) * 2 + core})

    def across():
        return remote(pair_out.at[2], pair_in.at[2], pair_sem, 2, {"tp": (y * 2 + 1 - z_lo) * 2 + core})

    def finish(i):
        sib_copy(i).wait_recv()
        both = part[lax.rem(i, 2)] + sib_in[i].astype(F32)

        @pl.when(lax.rem(i, 4) == 2)
        def _():
            kept[i // 4] = both

        @pl.when(lax.rem(i, 4) != 2)
        def _():
            pair_out[i] = both.astype(BF16)
            pair_copy(i).start()

    def reduce(i):
        chip = chunk_y(i) * 2 + jnp.where(i < 4, 1 - z_lo, z_lo)
        sib_out[i] = partial(block_rows(chip * 2 + 1 - core)).astype(BF16)
        sib_copy(i).start()
        part[lax.rem(i, 2)] = partial(block_rows(chip * 2 + core))

        @pl.when(i > 0)
        def _():
            finish(i - 1)

    loop(0, chips, reduce)
    finish(chips - 1)
    for i in range(2):
        spread_in(i).wait_recv()
        spread(i + 2).start()
    for i in (1, 2, 0):
        seq_gather.arrive(i)
    for i in (0, 3, 1):
        pair_copy(i).wait_recv()
    pair_out[2] = (
        kept[0] + pair_in[0].astype(F32) + pair_in[1].astype(F32) + pair_in[3].astype(F32)
    ).astype(BF16)
    across().start()

    stat_sib.wait_recv()
    stats[2] = stats[0] + stats[1]

    def stat_copy(k):
        return remote(stats.at[2], stats.at[2 + k], stat_sem, k, {"tp": tp_peer(k)})

    loop(1, chips, lambda k: stat_copy(k).start())

    def turn(chip):
        for half in range(2):
            cols_t[chip, half * own : half * own + own, :] = col[chip, half].T

    def product(source, begin=False):
        for j in range(3):
            term = jnp.dot(cols_t[source], gp_all[source, j], preferred_element_type=F32)
            total[j] = term if begin else total[j] + term

    for half in range(2):
        col[s, half] = ag[s * 2 + half, 0:tok, :]

    def pass_on(k):
        source = z_hi * 4 + lax.rem(x_at + k, 4)
        col_in(source).wait_recv()
        colf_copy(source).start()

    def turn_in(k):
        source = lax.rem(s + n_seq - k, n_seq)
        colf_in(source).wait_recv()
        turn(source)

    loop(1, 4, pass_on)
    turn(s)
    for i in (4, 3):
        seq_gather.arrive(i)
    for step in (0, -1, 1):
        colf_copy(fetched(step)).start()
    for i in (2, 3):
        spread_in(i).wait_recv()
    colf_copy(fetched(2)).start()
    loop(1, n_seq, turn_in)
    product(s, True)
    for i in (1, 2, 0, 4, 3):
        product(seq_gather.source(i))

    def collect(k):
        stat_copy(k).wait_recv()

    for i in (4, 5, 7):
        pair_copy(i).wait_recv()
    across().wait_recv()
    part[0] = (
        kept[1] + pair_in[4].astype(F32) + pair_in[5].astype(F32)
        + pair_in[7].astype(F32) + pair_in[2].astype(F32)
    )
    loop(1, chips, collect)
    stat_rows = sum(stats[2 + k] for k in range(chips)) * (1.0 / width)
    own_gain = ag[p, tok : tok + 16, :].astype(F32)[0:1]
    for h in range(tok // 128):
        r = slice(h * 128, h * 128 + 128)
        stat_col = jnp.sum(jnp.where(eye, stat_rows[h : h + 1, :], 0.0), axis=1, keepdims=True)
        rms = inv[r, 0:1]
        scaled = ag[p, r, :].astype(F32) * rms
        grad_in[r, :] = (rms * (own_gain * part[0, r, :] - scaled * stat_col)).astype(BF16)

    for i in (5, 6):
        product(seq_gather.arrive(i))
    for c in range(2 * own // 128):
        lane = (c * 128) % own
        g = ag[s * 2 + c * 128 // own, tok : tok + 16, lane : lane + 128].astype(F32)[0:1]
        g_col = jnp.sum(jnp.where(eye, g, 0.0), axis=1, keepdims=True)
        for j in range(3):
            grad_proj[j, c * 128 : c * 128 + 128, :] = (total[j, c * 128 : c * 128 + 128, :] * g_col).astype(BF16)

    def settle(k):
        @pl.when(k > 0)
        def _():
            stat_copy(k).wait_send()

        @pl.when(lax.rem(k, 4) != 2)
        def _():
            pair_copy(k).wait_send()

        sib_copy(k).wait_send()

        @pl.when(col_due(k))
        def _():
            col_send(k).wait_send()

        @pl.when(k != s)
        def _():
            colf_copy(k).wait_send()

    loop(0, chips, settle)
    across().wait_send()
    for i in range(4):
        spread(i).wait_send()
    for group in (gather, seq_gather):
        group.settle()
    for i in range(8):
        chip = q if i == 7 else gather.source(i)
        fwd_copy(i, chip).wait_send()
    stat_sib.wait_send()


def hand_over(*refs):
    for source, target in zip(refs[:3], refs[3:]):
        target[...] = source[...]


def per_device(activations, norm_gain, in_proj, short_taps, medium_taps, cotangent):
    tok, own = activations.shape
    width, _, ch = in_proj.shape
    n_seq, n_tp = lax.axis_size("seq"), lax.axis_size("tp")
    chips = n_tp // 2
    vmem = pl.BlockSpec(memory_space=pltpu.VMEM)
    hbm = pl.BlockSpec(memory_space=pl.ANY)
    sems = lambda count: pltpu.SemaphoreType.DMA((2, count))
    mix, grad_in, grad_proj = pl.pallas_call(
        whole_kernel,
        out_shape=(
            jax.ShapeDtypeStruct((tok, ch), BF16),
            jax.ShapeDtypeStruct((tok, own), BF16),
            jax.ShapeDtypeStruct((3, 2 * own, ch), BF16),
        ),
        in_specs=[hbm] * 3 + [vmem] * 3,
        out_specs=(vmem,) * 3,
        scratch_shapes=[
            pltpu.VMEM((n_tp, tok + 16, own), BF16),
            pltpu.VMEM((3, width, ch), BF16),
            pltpu.VMEM((3, tok, ch), F32),
            pltpu.VMEM((tok, 128), F32),
            pltpu.VMEM((tok, 128), F32),
            pltpu.VMEM((3, tok, ch), BF16),
            pltpu.VMEM((3, tok, ch), BF16),
            pltpu.VMEM((n_seq, 2, tok, own), BF16),
            pltpu.VMEM((n_seq, 2 * own, tok), BF16),
            pltpu.VMEM((n_seq, 3, tok, ch), BF16),
            pltpu.VMEM((3, 2 * own, ch), F32),
            pltpu.VMEM((chips, tok, own), BF16),
            pltpu.VMEM((chips, tok, own), BF16),
            pltpu.VMEM((chips, tok, own), BF16),
            pltpu.VMEM((chips, tok, own), BF16),
            pltpu.VMEM((2, tok, own), F32),
            pltpu.VMEM((2, tok, own), F32),
            pltpu.VMEM((2 + chips, 8, 128), F32),
            pltpu.SemaphoreType.DMA((2,)),
            pltpu.SemaphoreType.DMA((n_tp,)),
            sems(7), sems(8), sems(n_seq), sems(4), sems(n_seq), sems(7), sems(chips), sems(chips), sems(chips), sems(1),
        ] + mixer_scratch(tok, ch),
        compiler_params=pltpu.CompilerParams(
            collective_id=0, has_side_effects=True, vmem_limit_bytes=60 * 2**20
        ),
    )(
        activations,
        jnp.broadcast_to(norm_gain[None], (16, own)),
        jnp.transpose(in_proj, (1, 0, 2)),
        cotangent,
        short_taps,
        medium_taps,
    )
    results = (mix, grad_in, grad_proj)
    mix, grad_in, grad_proj = pl.pallas_call(
        hand_over,
        out_shape=tuple(jax.ShapeDtypeStruct(a.shape, a.dtype) for a in results),
        in_specs=[vmem] * 3,
        out_specs=(vmem,) * 3,
    )(*results)
    return mix, grad_in, jnp.transpose(grad_proj, (1, 0, 2))


def solution(mesh):
    return jax.shard_map(
        per_device,
        mesh=mesh,
        in_specs=(
            P("seq", "tp"), P("tp"), P(None, None, "tp"), P(None, None, "tp"), P("tp", None), P("seq", "tp"),
        ),
        out_specs=(P("seq", "tp"), P("seq", "tp"), P("seq", None, "tp")),
        check_vma=False,
    )
```

```python
import jax
import jax.numpy as jnp
from jax import lax
from jax.experimental import pallas as pl
from jax.experimental.pallas import tpu as pltpu
from jax.sharding import PartitionSpec as P

GROUP = 16
LM = 128
BLK = 128
EPS = 1e-06
F32 = jnp.float32
BF16 = jnp.bfloat16
MESH = pl.DeviceIdType.MESH


def build_bands(taps_ref, band_ref):
    groups = taps_ref.shape[0]

    def one(g, carry):
        row = jnp.broadcast_to(taps_ref[pl.ds(g, 1), :], (BLK, LM))
        wide = jnp.concatenate([row, jnp.zeros((BLK, BLK), F32)], 1)
        wide = pltpu.roll(wide, 0, 1, stride=1, stride_axis=0)
        band_ref[groups + g] = wide.astype(BF16)
        band_ref[g, :, 0:BLK] = wide[:, BLK:].T.astype(BF16)
        band_ref[g, :, BLK:] = wide[:, 0:BLK].T.astype(BF16)
        return carry

    lax.fori_loop(0, groups, one, 0)


def apply_band(band_ref, first, source_ref, row0):
    lane = lax.broadcasted_iota(jnp.int32, (BLK, 128), 1) // GROUP
    halves = source_ref.shape[1] // 128

    def one(g, totals):
        new = []
        for h in range(halves):
            part = jnp.dot(
                band_ref[first + h * 8 + g],
                source_ref[row0 : row0 + 2 * BLK, h * 128 : h * 128 + 128],
                preferred_element_type=F32,
            )
            new.append(jnp.where(lane == g, part, totals[h]))
        return tuple(new)

    totals = lax.fori_loop(0, 8, one, tuple(jnp.zeros((BLK, 128), F32) for _ in range(halves)))
    return jnp.concatenate(totals, 1)


def mixer(pre, cot, taps, band, mix, gp, ext, feat, gext, gfext, gft, ptail, ghead, gtail, send, recv):
    tok, ch = pre.shape[1], pre.shape[2]
    n = lax.axis_size("seq")
    me = lax.axis_index("seq")
    after, before = lax.rem(me + 1, n), lax.rem(me + n - 1, n)
    first, last = me == 0, me == n - 1
    groups = ch // GROUP

    def remote(src, dst, index, to):
        return pltpu.make_async_remote_copy(
            src_ref=src, dst_ref=dst, send_sem=send.at[index], recv_sem=recv.at[index],
            device_id={"seq": to}, device_id_type=MESH,
        )

    tail_copy = remote(pre.at[:, pl.ds(tok - 16, 16), :], ptail, 0, after)
    tail_copy.start()
    for j in range(3):
        ext[j, 8 : 8 + tok, :] = pre[j].astype(F32)

    def short(j, lo, hi):
        total = taps[0, j : j + 1, :] * ext[j, 8 + lo : 8 + hi, :]
        total += taps[1, j : j + 1, :] * ext[j, 7 + lo : 7 + hi, :]
        total += taps[2, j : j + 1, :] * ext[j, 6 + lo : 6 + hi, :]
        return total.astype(BF16)

    def gate(lo, hi):
        k, v = short(1, lo, hi), short(2, lo, hi)
        feat[1, lo:hi, :] = k
        feat[2, lo:hi, :] = v
        gext[BLK + lo : BLK + hi, :] = (k.astype(F32) * v.astype(F32)).astype(BF16)

    gate(tok - BLK, tok)
    gated_copy = remote(gext.at[pl.ds(tok, BLK), :], gext.at[pl.ds(0, BLK), :], 1, after)
    gated_copy.start()

    tail_copy.wait_recv()
    for j in range(3):
        ext[j, 0:8, :] = jnp.where(first, 0.0, ptail[j].astype(F32)[8:16])
    q = short(0, 0, tok)
    feat[0] = q
    grad_out = cot[...].astype(F32)
    gfext[0:tok, :] = (grad_out * q.astype(F32)).astype(BF16)
    filt_copy = remote(gfext.at[pl.ds(0, BLK), :], gtail, 2, before)
    filt_copy.start()
    gate(0, tok - BLK)

    def grad_kv(lo):
        gg = apply_band(band, groups, gfext, lo)
        gft[1, lo : lo + BLK, :] = (gg * feat[2, lo : lo + BLK, :].astype(F32)).astype(BF16).astype(F32)
        gft[2, lo : lo + BLK, :] = (gg * feat[1, lo : lo + BLK, :].astype(F32)).astype(BF16).astype(F32)

    def forward(lo):
        filt = apply_band(band, 0, gext, lo)
        mix[lo : lo + BLK, :] = (feat[0, lo : lo + BLK, :].astype(F32) * filt).astype(BF16)
        gft[0, lo : lo + BLK, :] = (cot[lo : lo + BLK, :].astype(F32) * filt).astype(BF16).astype(F32)

    grad_kv(0)
    gated_copy.wait_recv()

    @pl.when(first)
    def _():
        gext[0:BLK, :] = jnp.zeros((BLK, ch), BF16)

    forward(0)
    for j in range(3):
        ghead[0, j] = gft[j, 0:16, :].astype(BF16)
    head_copy = remote(ghead.at[0], ghead.at[1], 3, before)
    head_copy.start()
    forward(BLK)
    filt_copy.wait_recv()
    gfext[tok : tok + BLK, :] = jnp.where(last, 0.0, gtail[...].astype(F32)).astype(BF16)
    grad_kv(BLK)
    head_copy.wait_recv()
    for j in range(3):
        gft[j, tok : tok + 8, :] = jnp.where(last, 0.0, ghead[1, j].astype(F32)[0:8])
    for j in range(3):
        total = taps[0, j : j + 1, :] * gft[j, 0:tok, :]
        total += taps[1, j : j + 1, :] * gft[j, 1 : tok + 1, :]
        total += taps[2, j : j + 1, :] * gft[j, 2 : tok + 2, :]
        gp[j] = total.astype(BF16)
    for copy in (tail_copy, gated_copy, filt_copy, head_copy):
        copy.wait_send()


def mixer_scratch(tok, ch):
    return [
        pltpu.VMEM((2 * ch // GROUP, BLK, 2 * BLK), BF16),
        pltpu.VMEM((3, tok + 8, ch), F32),
        pltpu.VMEM((3, tok, ch), BF16),
        pltpu.VMEM((tok + BLK, ch), BF16),
        pltpu.VMEM((tok + BLK, ch), BF16),
        pltpu.VMEM((3, tok + 8, ch), F32),
        pltpu.VMEM((3, 16, ch), BF16),
        pltpu.VMEM((2, 3, 16, ch), BF16),
        pltpu.VMEM((BLK, ch), BF16),
        pltpu.SemaphoreType.DMA((4,)),
        pltpu.SemaphoreType.DMA((4,)),
    ]


class Gather:
    def __init__(self, ring, pair, block, slot, device, send, recv):
        self.ring, self.pair, self.block, self.slot, self.device = ring, pair, block, slot, device
        self.send, self.recv = send, recv

    def at(self, step, flip):
        ring = lax.rem(self.ring + step + 4, 4)
        return ring, (1 - self.pair if flip else self.pair)

    def source(self, i):
        where = ((0, 1), (-1, 0), (1, 0), (-1, 1), (1, 1), (2, 0), (2, 1))[i]
        return self.slot(*self.at(*where))

    def copy(self, i):
        what, to = (
            ((0, 0), (0, 1)), ((0, 0), (1, 0)), ((0, 0), (-1, 0)), ((0, 1), (1, 0)),
            ((0, 1), (-1, 0)), ((-1, 0), (1, 0)), ((1, 1), (-1, 0)),
        )[i]
        block = self.block(self.slot(*self.at(*what)))
        return pltpu.make_async_remote_copy(
            src_ref=block, dst_ref=block, send_sem=self.send.at[i], recv_sem=self.recv.at[i],
            device_id=self.device(*self.at(*to)), device_id_type=MESH,
        )

    def start(self):
        for i in range(3):
            self.copy(i).start()

    def arrive(self, i):
        block = self.block(self.source(i))
        pltpu.make_async_remote_copy(
            src_ref=block, dst_ref=block, send_sem=self.send.at[i], recv_sem=self.recv.at[i],
            device_id=self.device(*self.at(0, 1)), device_id_type=MESH,
        ).wait_recv()
        for following in {0: (3, 4), 1: (5,), 4: (6,)}.get(i, ()):
            self.copy(following).start()
        return self.source(i)

    def settle(self):
        for i in range(7):
            self.copy(i).wait_send()


def whole_kernel(
    act, gain, weight, cot, taps, medium, mix, grad_in, grad_proj,
    ag, w, acc, ssq, inv, pre, gp, col, cols_t, gp_all, total, sib_out, sib_in, pair_out, pair_in, part, kept, stats,
    load_sem, w_sem, ag_sem, fwd_sem, col_sem, spread_sem, colf_sem, gp_sem, sib_sem, pair_sem, stat_sem, statp_sem,
    band, *halo,
):
    n_seq, n_tp = lax.axis_size("seq"), lax.axis_size("tp")
    tok, own = act.shape
    ch = pre.shape[2]
    chips = n_tp // 2
    s, p = lax.axis_index("seq"), lax.axis_index("tp")
    q, core = p // 2, lax.rem(p, 2)
    sib = p + 1 - 2 * core
    width = n_tp * own

    def remote(src, dst, sems, index, to):
        return pltpu.make_async_remote_copy(
            src_ref=src, dst_ref=dst, send_sem=sems.at[0, index], recv_sem=sems.at[1, index],
            device_id=to, device_id_type=MESH,
        )

    def tp_peer(k):
        return lax.rem(q + k, chips) * 2 + core

    def loop(lo, hi, body):
        def step(i, carry):
            body(i)
            return carry

        lax.fori_loop(lo, hi, step, 0)

    def block_rows(index):
        return pl.ds(pl.multiple_of(index * own, own), own)

    loads = (
        pltpu.make_async_copy(act, ag.at[p, pl.ds(0, tok), :], load_sem.at[0]),
        pltpu.make_async_copy(gain, ag.at[p, pl.ds(tok, 16), :], load_sem.at[1]),
    )
    for copy in loads:
        copy.start()

    def w_copy(index):
        return pltpu.make_async_copy(
            weight.at[:, block_rows(index), :], w.at[:, block_rows(index), :], w_sem.at[index]
        )

    loop(0, n_tp, lambda i: w_copy(lax.rem(p + i, n_tp)).start())

    barrier = pltpu.get_barrier_semaphore()

    def greet(k):
        pl.semaphore_signal(barrier, inc=1, device_id={"seq": s, "tp": tp_peer(k)}, device_id_type=MESH)
        to = lax.rem(s + k, n_seq)
        pl.semaphore_signal(barrier, inc=1, device_id={"seq": to, "tp": p}, device_id_type=MESH)

    loop(1, 8, greet)
    pl.semaphore_signal(barrier, inc=1, device_id={"seq": s, "tp": sib}, device_id_type=MESH)

    for copy in loads:
        copy.wait()
    pl.semaphore_wait(barrier, 15)

    y, z_lo = q // 2, lax.rem(q, 2)
    gather = Gather(
        y, z_lo, lambda chip: ag.at[chip * 2 + core], lambda r, z: r * 2 + z,
        lambda r, z: {"tp": (r * 2 + z) * 2 + core}, ag_sem.at[0], ag_sem.at[1],
    )
    gather.start()

    z_hi, x_at = s // 4, lax.rem(s, 4)
    def col_send(to):
        return pltpu.make_async_remote_copy(
            src_ref=ag.at[to * 2 + core, pl.ds(0, tok), :], dst_ref=col.at[s, core],
            send_sem=col_sem.at[0, to], recv_sem=col_sem.at[1, s],
            device_id={"seq": to}, device_id_type=MESH,
        )

    def col_in(source):
        return pltpu.make_async_remote_copy(
            src_ref=col.at[source, core], dst_ref=col.at[source, core],
            send_sem=col_sem.at[0, source], recv_sem=col_sem.at[1, source],
            device_id={"seq": source}, device_id_type=MESH,
        )

    def col_due(chip):
        near = chip // 4 == z_hi
        return (near & (lax.rem(chip, 4) != x_at)) | (~near & (lax.rem(chip + y, 4) == x_at))

    def col_start(chip):
        @pl.when(col_due(chip))
        def _():
            col_send(chip).start()

    def fetched(step):
        return (1 - z_hi) * 4 + lax.rem(x_at + y + step + 4, 4)

    def spread(i):
        step, part_rows, to = (
            (0, pl.ds(0, tok), 1), (0, pl.ds(0, tok), 3), (-1, pl.ds(0, tok // 2), 1), (1, pl.ds(tok // 2, tok // 2), 3),
        )[i]
        block = col.at[fetched(step), core, part_rows, :]
        return remote(block, block, spread_sem, i, {"tp": (lax.rem(y + to, 4) * 2 + z_lo) * 2 + core})

    def spread_in(i):
        step, part_rows = (
            (-1, pl.ds(0, tok)), (1, pl.ds(0, tok)), (2, pl.ds(0, tok // 2)), (2, pl.ds(tok // 2, tok // 2)),
        )[i]
        block = col.at[fetched(step), core, part_rows, :]
        return remote(block, block, spread_sem, i, {"tp": sib})

    def fwd_copy(i, chip):
        slot = chip * 2 + core
        return remote(ag.at[slot], ag.at[slot], fwd_sem, i, {"tp": sib})

    def fwd_in(i, chip):
        slot = chip * 2 + 1 - core
        return remote(ag.at[slot], ag.at[slot], fwd_sem, i, {"tp": sib})

    def colf_copy(source):
        return remote(col.at[source, core], col.at[source, core], colf_sem, source, {"tp": sib})

    def colf_in(source):
        return remote(col.at[source, 1 - core], col.at[source, 1 - core], colf_sem, source, {"tp": sib})

    fwd_copy(7, q).start()
    build_bands(medium, band)
    acc[...] = jnp.zeros_like(acc)
    ssq[...] = jnp.zeros_like(ssq)

    def absorb(slot):
        w_copy(slot).wait()
        x = ag[slot, 0:tok, :].astype(F32)
        g = ag[slot, tok : tok + 16, :].astype(F32)[0:1]
        square = x * x
        ssq[...] += sum(square[:, i * 128 : i * 128 + 128] for i in range(own // 128))
        scaled = (x * g).astype(BF16)
        for j in range(3):
            acc[j] += jnp.dot(scaled, w[j, block_rows(slot), :], preferred_element_type=F32)

    def absorb_both(i, chip):
        absorb(chip * 2 + core)
        fwd_in(i, chip).wait_recv()
        absorb(chip * 2 + 1 - core)

    def take(i):
        chip = gather.arrive(i)
        fwd_copy(i, chip).start()
        col_start(chip)
        return chip

    absorb_both(7, q)
    for batch in ((0, 1, 2), (4, 3)):
        chips_in = [take(i) for i in batch]
        if 0 in batch:
            col_start(q)
        for i, chip in zip(batch, chips_in):
            absorb_both(i, chip)

    five = take(5)
    six = take(6)
    absorb_both(5, five)
    absorb_both(6, six)

    inv[...] = jnp.broadcast_to(
        lax.rsqrt(jnp.sum(ssq[...], axis=1, keepdims=True) * (1.0 / width) + EPS), inv.shape
    )
    for j in range(3):
        pre[j] = (acc[j] * inv[:, 0:1]).astype(BF16)

    mixer(
        pre, cot, taps, band, mix, gp, *halo,
    )

    seq_gather = Gather(
        lax.rem(s, 4), s // 4, lambda slot: gp_all.at[slot], lambda r, z: z * 4 + r,
        lambda r, z: {"seq": z * 4 + r}, gp_sem.at[0], gp_sem.at[1],
    )
    stat = jnp.zeros((tok, ch), F32)
    for j in range(3):
        value = gp[j].astype(F32)
        gp_all[s, j] = (value * inv[:, 0:1]).astype(BF16)
        stat += value * pre[j].astype(F32)
    seq_gather.start()
    col_in(fetched(0)).wait_recv()
    for i in range(2):
        spread(i).start()


    eye = lax.broadcasted_iota(jnp.int32, (128, 128), 0) == lax.broadcasted_iota(jnp.int32, (128, 128), 1)

    stat = jnp.sum(stat, axis=1, keepdims=True)
    stats[0] = jnp.zeros((8, 128), F32)
    for h in range(tok // 128):
        piece = jnp.where(eye, stat[h * 128 : h * 128 + 128], 0.0)
        stats[0, h : h + 1, :] = jnp.sum(piece, axis=0, keepdims=True)
    stat_sib = remote(stats.at[0], stats.at[1], statp_sem, 0, {"tp": sib})
    stat_sib.start()

    def partial(rows_):
        value = None
        for j in range(3):
            term = lax.dot_general(
                gp[j], w[j, rows_, :], (((1,), (1,)), ((), ())), preferred_element_type=F32
            )
            value = term if value is None else value + term
        return value

    def sib_copy(i):
        return remote(sib_out.at[i], sib_in.at[i], sib_sem, i, {"tp": sib})

    def chunk_y(i):
        return lax.rem(y + 2 + i, 4)

    def pair_copy(i):
        return remote(pair_out.at[i], pair_in.at[i], pair_sem, i, {"tp": (chunk_y(i) * 2 + z_lo) * 2 + core})

    def across():
        return remote(pair_out.at[2], pair_in.at[2], pair_sem, 2, {"tp": (y * 2 + 1 - z_lo) * 2 + core})

    def finish(i):
        sib_copy(i).wait_recv()
        both = part[lax.rem(i, 2)] + sib_in[i].astype(F32)

        @pl.when(lax.rem(i, 4) == 2)
        def _():
            kept[i // 4] = both

        @pl.when(lax.rem(i, 4) != 2)
        def _():
            pair_out[i] = both.astype(BF16)
            pair_copy(i).start()

    def reduce(i):
        chip = chunk_y(i) * 2 + jnp.where(i < 4, 1 - z_lo, z_lo)
        sib_out[i] = partial(block_rows(chip * 2 + 1 - core)).astype(BF16)
        sib_copy(i).start()
        part[lax.rem(i, 2)] = partial(block_rows(chip * 2 + core))

        @pl.when(i > 0)
        def _():
            finish(i - 1)

    loop(0, chips, reduce)
    finish(chips - 1)
    for i in range(2):
        spread_in(i).wait_recv()
        spread(i + 2).start()
    for i in (1, 2, 0):
        seq_gather.arrive(i)
    for i in (0, 3, 1):
        pair_copy(i).wait_recv()
    pair_out[2] = (
        kept[0] + pair_in[0].astype(F32) + pair_in[1].astype(F32) + pair_in[3].astype(F32)
    ).astype(BF16)
    across().start()

    stat_sib.wait_recv()
    stats[2] = stats[0] + stats[1]

    def stat_copy(k):
        return remote(stats.at[2], stats.at[2 + k], stat_sem, k, {"tp": tp_peer(k)})

    loop(1, chips, lambda k: stat_copy(k).start())

    def turn(chip):
        for half in range(2):
            cols_t[chip, half * own : half * own + own, :] = col[chip, half].T

    def product(source, begin=False):
        for j in range(3):
            term = jnp.dot(cols_t[source], gp_all[source, j], preferred_element_type=F32)
            total[j] = term if begin else total[j] + term

    for half in range(2):
        col[s, half] = ag[s * 2 + half, 0:tok, :]

    def pass_on(k):
        source = z_hi * 4 + lax.rem(x_at + k, 4)
        col_in(source).wait_recv()
        colf_copy(source).start()

    def turn_in(k):
        source = lax.rem(s + n_seq - k, n_seq)
        colf_in(source).wait_recv()
        turn(source)

    loop(1, 4, pass_on)
    turn(s)
    for i in (4, 3):
        seq_gather.arrive(i)
    for step in (0, -1, 1):
        colf_copy(fetched(step)).start()
    for i in (2, 3):
        spread_in(i).wait_recv()
    colf_copy(fetched(2)).start()
    loop(1, n_seq, turn_in)
    product(s, True)
    for i in (1, 2, 0, 4, 3):
        product(seq_gather.source(i))

    def collect(k):
        stat_copy(k).wait_recv()

    for i in (4, 5, 7):
        pair_copy(i).wait_recv()
    across().wait_recv()
    part[0] = (
        kept[1] + pair_in[4].astype(F32) + pair_in[5].astype(F32)
        + pair_in[7].astype(F32) + pair_in[2].astype(F32)
    )
    loop(1, chips, collect)
    stat_rows = sum(stats[2 + k] for k in range(chips)) * (1.0 / width)
    own_gain = ag[p, tok : tok + 16, :].astype(F32)[0:1]
    for h in range(tok // 128):
        r = slice(h * 128, h * 128 + 128)
        stat_col = jnp.sum(jnp.where(eye, stat_rows[h : h + 1, :], 0.0), axis=1, keepdims=True)
        rms = inv[r, 0:1]
        scaled = ag[p, r, :].astype(F32) * rms
        grad_in[r, :] = (rms * (own_gain * part[0, r, :] - scaled * stat_col)).astype(BF16)

    for i in (5, 6):
        product(seq_gather.arrive(i))
    for c in range(2 * own // 128):
        lane = (c * 128) % own
        g = ag[s * 2 + c * 128 // own, tok : tok + 16, lane : lane + 128].astype(F32)[0:1]
        g_col = jnp.sum(jnp.where(eye, g, 0.0), axis=1, keepdims=True)
        for j in range(3):
            grad_proj[j, c * 128 : c * 128 + 128, :] = (total[j, c * 128 : c * 128 + 128, :] * g_col).astype(BF16)

    def settle(k):
        @pl.when(k > 0)
        def _():
            stat_copy(k).wait_send()

        @pl.when(lax.rem(k, 4) != 2)
        def _():
            pair_copy(k).wait_send()

        sib_copy(k).wait_send()

        @pl.when(col_due(k))
        def _():
            col_send(k).wait_send()

        @pl.when(k != s)
        def _():
            colf_copy(k).wait_send()

    loop(0, chips, settle)
    across().wait_send()
    for i in range(4):
        spread(i).wait_send()
    for group in (gather, seq_gather):
        group.settle()
    for i in range(8):
        chip = q if i == 7 else gather.source(i)
        fwd_copy(i, chip).wait_send()
    stat_sib.wait_send()


def hand_over(*refs):
    for source, target in zip(refs[:3], refs[3:]):
        target[...] = source[...]


def per_device(activations, norm_gain, in_proj, short_taps, medium_taps, cotangent):
    tok, own = activations.shape
    width, _, ch = in_proj.shape
    n_seq, n_tp = lax.axis_size("seq"), lax.axis_size("tp")
    chips = n_tp // 2
    vmem = pl.BlockSpec(memory_space=pltpu.VMEM)
    hbm = pl.BlockSpec(memory_space=pl.ANY)
    sems = lambda count: pltpu.SemaphoreType.DMA((2, count))
    mix, grad_in, grad_proj = pl.pallas_call(
        whole_kernel,
        out_shape=(
            jax.ShapeDtypeStruct((tok, ch), BF16),
            jax.ShapeDtypeStruct((tok, own), BF16),
            jax.ShapeDtypeStruct((3, 2 * own, ch), BF16),
        ),
        in_specs=[hbm] * 3 + [vmem] * 3,
        out_specs=(vmem,) * 3,
        scratch_shapes=[
            pltpu.VMEM((n_tp, tok + 16, own), BF16),
            pltpu.VMEM((3, width, ch), BF16),
            pltpu.VMEM((3, tok, ch), F32),
            pltpu.VMEM((tok, 128), F32),
            pltpu.VMEM((tok, 128), F32),
            pltpu.VMEM((3, tok, ch), BF16),
            pltpu.VMEM((3, tok, ch), BF16),
            pltpu.VMEM((n_seq, 2, tok, own), BF16),
            pltpu.VMEM((n_seq, 2 * own, tok), BF16),
            pltpu.VMEM((n_seq, 3, tok, ch), BF16),
            pltpu.VMEM((3, 2 * own, ch), F32),
            pltpu.VMEM((chips, tok, own), BF16),
            pltpu.VMEM((chips, tok, own), BF16),
            pltpu.VMEM((chips, tok, own), BF16),
            pltpu.VMEM((chips, tok, own), BF16),
            pltpu.VMEM((2, tok, own), F32),
            pltpu.VMEM((2, tok, own), F32),
            pltpu.VMEM((2 + chips, 8, 128), F32),
            pltpu.SemaphoreType.DMA((2,)),
            pltpu.SemaphoreType.DMA((n_tp,)),
            sems(7), sems(8), sems(n_seq), sems(4), sems(n_seq), sems(7), sems(chips), sems(chips), sems(chips), sems(1),
        ] + mixer_scratch(tok, ch),
        compiler_params=pltpu.CompilerParams(
            collective_id=0, has_side_effects=True, vmem_limit_bytes=60 * 2**20
        ),
    )(
        activations,
        jnp.broadcast_to(norm_gain[None], (16, own)),
        jnp.transpose(in_proj, (1, 0, 2)),
        cotangent,
        short_taps,
        medium_taps,
    )
    results = (mix, grad_in, grad_proj)
    mix, grad_in, grad_proj = pl.pallas_call(
        hand_over,
        out_shape=tuple(jax.ShapeDtypeStruct(a.shape, a.dtype) for a in results),
        in_specs=[vmem] * 3,
        out_specs=(vmem,) * 3,
    )(*results)
    return mix, grad_in, jnp.transpose(grad_proj, (1, 0, 2))


def solution(mesh):
    return jax.shard_map(
        per_device,
        mesh=mesh,
        in_specs=(
            P("seq", "tp"), P("tp"), P(None, None, "tp"), P(None, None, "tp"), P("tp", None), P("seq", "tp"),
        ),
        out_specs=(P("seq", "tp"), P("seq", "tp"), P("seq", None, "tp")),
        check_vma=False,
    )
```
